256 devices in a mesh: zg: 16 (over y, z_hi), xy: 16 (over x, z_lo, core).
Axes of the slice: x: 4, y: 4, z: 8 (z_hi: 4, z_lo: 2; z = z_hi * 2 + z_lo), core: 2. Of those that a mesh axis runs over, the one named last changes fastest.
Arguments:
- start_field: float32 [192, 128, 1024], P('zg', 'xy'), may hold values from -6 to 6
- diffusivity: float32 [192, 128, 1024], P('zg', 'xy'), may hold values from 0.02 to 0.13
- tile_block: int32 [192, 128, 16], P('zg', 'xy'), may hold values from 0 to 4096, as said below
- block_material: int32 [4096], replicated, may hold values from 0 to 1
- material_coupling: float32 [2, 64, 64], replicated, as said below
Outputs:
- final_field: float32 [192, 128, 1024], P('zg', 'xy')
The draws below stay inside these ranges and needn't reach their ends.
Inputs may be any that keep to these rules, and one draw needn't show every extreme that they name: `tile_block`: 0 marks a tile outside every inclusion; k > 0 names inclusion block k - 1. `block_material`: an index into material_coupling. `material_coupling`: each material's coupling among the 64 cells of a tile.
All inputs are finite; a program needn't handle non-finite values.
Results may differ from the reference program's by a relative error of at most 0.0003.
Values sent between devices are 32-bit elements; how exact they have to be, the bound alone decides.
No kernel may reach another device: no remote copies, remote signals or barrier semaphores. Data moves between devices by JAX's collectives and lax.ppermute only.
A program may use at most 64 MiB of HBM per device.

```python
import math
import jax
import jax.numpy as jnp
from jax import lax

CZ = 12
NY = 1024
TILE = 64
MATS = 2
BLOCKS = 4096
STEPS = 8
ITERS = 2
NZ = 192
NX = 128
TILES = 16
N_ZG = 16


def draw_tile_block(key, part):
    key = jax.random.fold_in(key, 11)
    first_key, second_key = jax.random.split(key)
    occupied = jax.random.randint(first_key, (NZ, NX, TILES), 0, 2)
    which = jax.random.randint(second_key, (NZ, NX, TILES), 1, BLOCKS + 1)
    table = occupied * which
    table = table.at[0, 0, 0].set(BLOCKS)
    table = table.at[0, 0, 1].set(0)
    return table.astype(jnp.int32)


def draw_material_coupling(key, part):
    key = jax.random.fold_in(key, 23)
    first_key, second_key = jax.random.split(key)
    strength = jnp.where(jnp.arange(MATS) == 0, 0.08, 0.2).astype(jnp.float32)[:, None, None]
    diagonal = jax.random.uniform(first_key, (MATS, TILE), jnp.float32, 0.6, 1.4)
    spread = jax.random.normal(second_key, (MATS, TILE, TILE), jnp.float32)
    identity = jnp.eye(TILE, dtype=jnp.float32)
    return strength * (identity * diagonal[:, :, None] + (1.0 - identity) * spread * 0.03)


def plant(array, stream_key, smallest, largest):
    longest = array.shape.index(max(array.shape))
    spots = []
    for shift in (0, 1):
        where = [jax.random.randint(jax.random.fold_in(stream_key, axis), (), 0, length) for axis, length in enumerate(array.shape)]
        where[longest] = (where[longest] + shift) % array.shape[longest]
        spots.append(tuple(where))
    return array.at[spots[0]].set(smallest).at[spots[1]].set(largest)


def level_of(stream_key, dims, shards, least, largest):
    gain = 1.0
    for axis_at, blocks in shards:
        heights = jax.random.uniform(jax.random.fold_in(jax.random.fold_in(stream_key, 6), axis_at), (blocks,), jnp.float32, least / len(shards), largest / len(shards))
        gain = gain * jnp.repeat(jnp.exp(heights), dims[axis_at] // blocks).reshape((-1,) + (1,) * (len(dims) - 1 - axis_at))
    return gain


def bell_draw(rng, shape, scale, limit, cuts=(), held_as=jnp.bfloat16):
    level = level_of(rng, shape, cuts, -0.22, 0.18) if cuts else 1.0
    result = jax.random.normal(rng, shape, jnp.float32) * scale * level
    return jnp.minimum(jnp.maximum(result, -limit), limit).astype(held_as)


def setup_inputs(seed: int = 0) -> dict:
    streams_of = jax.random.split(jax.random.key(seed), 6)
    return {
        "start_field": bell_draw(streams_of[0], (NZ, NX, NY), 1.0, 6.0, ((0, 16), (1, 16)), jnp.float32),
        "diffusivity": jnp.clip(jnp.exp(math.log(0.13) - 1.8718022 * jax.random.uniform(streams_of[1], (NZ, NX, NY), jnp.float32) ** level_of(streams_of[1], (NZ, NX, NY), ((0, 16), (1, 16)), -0.2, 0.2)), 0.02, 0.13),
        "tile_block": draw_tile_block(jax.random.fold_in(streams_of[5], 71), 0),
        "block_material": plant(jax.random.randint(streams_of[3], (BLOCKS,), 0, MATS), jax.random.fold_in(streams_of[3], 1), 0, MATS - 1).astype(jnp.int32),
        "material_coupling": draw_material_coupling(jax.random.fold_in(streams_of[5], 71), 0),
    }


def trace_value(nearer, farther):
    return (farther - nearer) + 0.25 * (3.0 * nearer - farther)


def ghost_value(robin_data, edge_plane):
    return (robin_data + 0.75 * edge_plane) / 1.25


def tile_codes(tile_block, block_material):
    looked = jnp.take(block_material, jnp.maximum(tile_block - 1, 0).astype(jnp.int32), axis=0)
    return jnp.where(tile_block > 0, looked + 1, 0).astype(jnp.int32)


def penalty_plane(plane, tile_code, joined):
    tile_rows = plane.reshape(-1, TILE)
    product = jnp.dot(tile_rows, joined, precision=lax.Precision.HIGHEST, preferred_element_type=jnp.float32)
    mark_column = tile_code.reshape(-1, 1)
    picked = jnp.where(mark_column == 1, product[:, :TILE], 0.0) + jnp.where(mark_column == 2, product[:, TILE:], 0.0)
    return picked.reshape(plane.shape)


def advance(current, conduct, tile_code, joined, below_data, above_data):
    below_ghost = ghost_value(below_data, current[:, 0])
    above_ghost = ghost_value(above_data, current[:, -1])
    upper_plane = jnp.concatenate([current[:, 1:], above_ghost[:, None]], axis=1)
    lower_plane = jnp.concatenate([below_ghost[:, None], current[:, :-1]], axis=1)
    padded_across = jnp.pad(current, ((0, 0), (0, 0), (1, 1), (0, 0)))
    padded_span = jnp.pad(current, ((0, 0), (0, 0), (0, 0), (1, 1)))
    laplace = (upper_plane + lower_plane + padded_across[:, :, 2:] + padded_across[:, :, :-2]
               + padded_span[..., 2:] + padded_span[..., :-2] - 6.0 * current)
    planes = current.reshape(-1, NX, NY)
    plane_codes = tile_code.reshape(-1, NX, TILES)
    penalty = lax.map(lambda bundle: penalty_plane(bundle[0], bundle[1], joined), (planes, plane_codes))
    return current + conduct * laplace - penalty.reshape(current.shape)


def reference(start_field, diffusivity, tile_block, block_material, material_coupling):
    tile_code = tile_codes(tile_block, block_material)
    joined = jnp.concatenate([material_coupling[0].T, material_coupling[1].T], axis=1)
    initial = start_field.reshape(N_ZG, CZ, NX, NY)
    conduct = diffusivity.reshape(N_ZG, CZ, NX, NY)
    blank_plane = jnp.zeros((N_ZG, NX, NY), jnp.float32)
    below_list = [blank_plane] * STEPS
    above_list = [blank_plane] * STEPS
    current = initial
    for iteration in range(ITERS):
        current = initial
        next_below = []
        next_above = []
        for moment in range(STEPS):
            if iteration + 1 < ITERS:
                upward = trace_value(current[:, -1], current[:, -2])
                downward = trace_value(current[:, 0], current[:, 1])
                next_below.append(jnp.concatenate([blank_plane[:1], upward[:-1]], axis=0))
                next_above.append(jnp.concatenate([downward[1:], blank_plane[:1]], axis=0))
            current = advance(current, conduct, tile_code, joined, below_list[moment], above_list[moment])
        below_list = next_below
        above_list = next_above
    return current.reshape(NZ, NX, NY)
```

```python
import jax
import jax.numpy as jnp
from jax import lax
from jax.experimental import pallas as pl
from jax.experimental.pallas import tpu as pltpu
from jax.sharding import PartitionSpec as P

TILE = 64
STEPS = 8
PLANES = 12
OWN = 8
HALO = 8
ROWS = OWN + 2 * HALO
SUB = 8
LANES = 128
CHUNKS = 8
VMEM_LIMIT = 48 * 1024 * 1024


def trace_rows(level):
    return 1 + level, ROWS - 1 - level


TRACE_AT = [0]
for _level in range(STEPS):
    _low, _high = trace_rows(_level)
    TRACE_AT.append(TRACE_AT[-1] + (_high - _low) * SUB)

KEPT = [(level, plane) for level in range(6) for plane in sorted({level, level + 1, 10 - level, 11 - level})]
KEPT_AT = {pair: i for i, pair in enumerate(KEPT)}


def span_sum(cells):
    lane = lax.broadcasted_iota(jnp.int32, (1, SUB, LANES), 2)
    row = lax.broadcasted_iota(jnp.int32, (1, SUB, LANES), 1)
    first = lane == 0
    last = lane == LANES - 1
    corner = (first & (row == 0)) | (last & (row == SUB - 1))
    after = pltpu.roll(cells, LANES - 1, 2)
    before = pltpu.roll(cells, 1, 2)
    carry = jnp.where(last, pltpu.roll(after, SUB - 1, 1), pltpu.roll(before, 1, 1))
    carry = jnp.where(corner, 0.0, carry)
    return jnp.where(last, carry, after) + jnp.where(first, carry, before)


def split_cells(values):
    high = values.astype(jnp.bfloat16)
    low = (values - high.astype(jnp.float32)).astype(jnp.bfloat16)
    return high, low


def weights(couple_ref):
    high, low = split_cells(couple_ref[...])
    return jnp.concatenate([high, high, low], axis=0)


def advance(src, dst, conduct, code, weight, first, count, low, high):
    rows = high - low
    at = pl.ds(low * SUB, rows * SUB)
    mid = pl.ds(first + 1, count)
    here = src[mid, at, :]
    around = (
        src[pl.ds(first, count), at, :]
        + src[pl.ds(first + 2, count), at, :]
        + src[mid, pl.ds((low - 1) * SUB, rows * SUB), :]
        + src[mid, pl.ds((low + 1) * SUB, rows * SUB), :]
    )
    along = span_sum(here.reshape(count * rows, SUB, LANES)).reshape(here.shape)
    flat = here.reshape(count * rows * SUB, LANES)
    near, rest = split_cells(flat)
    product = jnp.dot(
        jnp.concatenate([near, rest, near], axis=1), weight, preferred_element_type=jnp.float32
    )
    plane = pl.ds(first, count)
    marks = code[plane, at, :]
    penalty = jnp.where(
        marks == 1.0,
        product[:, :LANES].reshape(here.shape),
        jnp.where(marks == 2.0, product[:, LANES:].reshape(here.shape), 0.0),
    )
    dst[mid, at, :] = here + conduct[plane, at, :] * (around + along - 6.0 * here) - penalty


def advance_groups(src, dst, conduct, code, weight, groups, count, stride, low, high):
    def body(i, carry):
        advance(src, dst, conduct, code, weight, i * stride, count, low, high)
        return carry

    if groups == 1:
        advance(src, dst, conduct, code, weight, 0, count, low, high)
    else:
        lax.fori_loop(0, groups, body, 0)


def spread(block, dst, offset, at_plane):
    for plane in range(PLANES):
        for chunk in range(CHUNKS):
            dst[plane + at_plane, pl.ds(offset * SUB + chunk, OWN, stride=SUB), :] = block[
                plane, :, chunk * LANES : (chunk + 1) * LANES
            ]


def mark_cells(tile_ref, material_ref, wide, dst, offset):
    table = material_ref[...]
    row = lax.broadcasted_iota(jnp.int32, (SUB, LANES), 0)
    bits = jnp.zeros((SUB, LANES), jnp.int32)
    for part in range(table.shape[0] // SUB):
        bits = bits + (table[part * SUB : (part + 1) * SUB] << (row + part * SUB))
    for shift in (4, 2, 1):
        bits = bits + pltpu.roll(bits, shift, 0)
    tile_of = lax.broadcasted_iota(jnp.int32, (LANES, CHUNKS * LANES), 0)
    cell_of = lax.broadcasted_iota(jnp.int32, (LANES, CHUNKS * LANES), 1)
    widen = jnp.where(tile_of == cell_of // TILE, 1.0, 0.0).astype(jnp.bfloat16)
    parts = []
    for plane in range(PLANES):
        block = tile_ref[plane]
        entry = jnp.maximum(block - 1, 0)
        word = jnp.take_along_axis(bits, entry & (LANES - 1), axis=1)
        kind = (word >> (entry >> 7)) & 1
        parts.append(jnp.where(block > 0, kind + 1, 0).astype(jnp.float32))
    codes = jnp.concatenate(parts, axis=0).astype(jnp.bfloat16)
    wide[...] = jnp.dot(codes, widen, preferred_element_type=jnp.float32).reshape(wide.shape)
    spread(wide, dst, offset, 0)


def first_kernel(
    own_v, left_v, right_v, own_d, left_d, right_d, own_t, left_t, right_t, material, couple,
    to_below, to_above, kept, conduct, code,
    even, odd, wide,
):
    weight = weights(couple)
    for offset, cells, factor, tiles in (
        (0, left_v, left_d, left_t),
        (HALO, own_v, own_d, own_t),
        (HALO + OWN, right_v, right_d, right_t),
    ):
        spread(cells, even, offset, 1)
        spread(factor, conduct, offset, 0)
        mark_cells(tiles, material, wide, code, offset)
    buffers = (even, odd)
    for level in range(STEPS):
        src, dst = buffers[level % 2], buffers[1 - level % 2]
        low, high = trace_rows(level)
        at = pl.ds(low * SUB, (high - low) * SUB)
        place = pl.ds(TRACE_AT[level], (high - low) * SUB)
        to_below[place, :] = 0.75 * src[2, at, :] - 0.25 * src[1, at, :]
        to_above[place, :] = 0.75 * src[PLANES - 1, at, :] - 0.25 * src[PLANES, at, :]
        for plane in range(PLANES):
            if (level, plane) in KEPT_AT:
                wider = pl.ds((low - 1) * SUB, (high - low + 2) * SUB)
                kept[KEPT_AT[level, plane], wider, :] = src[plane + 1, wider, :]
        if level == STEPS - 1:
            break
        if level >= 5:
            low, high = low + 1, high - 1
        at = pl.ds(low * SUB, (high - low) * SUB)
        src[0, at, :] = src[1, at, :] * 0.6
        src[PLANES + 1, at, :] = src[PLANES, at, :] * 0.6
        groups, count, stride = {5: (2, 3, 9), 6: (2, 2, 10)}.get(level, (3, 4, 4))
        advance_groups(src, dst, conduct, code, weight, groups, count, stride, low, high)


def second_kernel(from_below, from_above, kept, conduct, code, couple, result, even, odd):
    weight = weights(couple)
    buffers = (even, odd)
    for level in range(STEPS):
        src, dst = buffers[level % 2], buffers[1 - level % 2]
        low, high = trace_rows(level)
        wider = pl.ds((low - 1) * SUB, (high - low + 2) * SUB)
        for plane in range(PLANES):
            if (level, plane) in KEPT_AT:
                src[plane + 1, wider, :] = kept[KEPT_AT[level, plane], wider, :]
        at = pl.ds(low * SUB, (high - low) * SUB)
        place = pl.ds(TRACE_AT[level], (high - low) * SUB)
        src[0, at, :] = (from_below[place, :] + 0.75 * src[1, at, :]) * 0.8
        src[PLANES + 1, at, :] = (from_above[place, :] + 0.75 * src[PLANES, at, :]) * 0.8
        groups, count, stride = (2, level + 1, 11 - level) if level < 5 else (3, 4, 4)
        advance_groups(src, dst, conduct, code, weight, groups, count, stride, low, high)
    final = buffers[STEPS % 2]
    for plane in range(PLANES):
        for chunk in range(CHUNKS):
            result[plane, :, chunk * LANES : (chunk + 1) * LANES] = final[
                plane + 1, pl.ds(HALO * SUB + chunk, OWN, stride=SUB), :
            ]


def shape(*dims):
    return jax.ShapeDtypeStruct(dims, jnp.float32)


VMEM = pl.BlockSpec(memory_space=pltpu.VMEM)
FIELD = (PLANES, ROWS * SUB, LANES)
PADDED = (PLANES + 2, ROWS * SUB, LANES)


def neighbours(cells, axis):
    ends = lax.axis_size(axis) - 1
    return (
        lax.ppermute(cells, axis, [(i, i + 1) for i in range(ends)]),
        lax.ppermute(cells, axis, [(i + 1, i) for i in range(ends)]),
    )


def on_device(start_field, diffusivity, tile_block, block_material, material_coupling):
    tiles = jnp.pad(tile_block, ((0, 0), (0, 0), (0, LANES - tile_block.shape[2])))
    left_t, right_t = neighbours(tiles, "xy")
    left_v, right_v = neighbours(start_field, "xy")
    left_d, right_d = neighbours(diffusivity, "xy")
    turned = jnp.swapaxes(material_coupling, 1, 2)
    empty = jnp.zeros((TILE, TILE), jnp.float32)
    couple = jnp.concatenate(
        [jnp.block([[turned[kind], empty], [empty, turned[kind]]]) for kind in (0, 1)], axis=1
    )
    material = block_material.reshape(-1, LANES)
    to_below, to_above, kept, conduct, code = pl.pallas_call(
        first_kernel,
        out_shape=[
            shape(TRACE_AT[-1], LANES),
            shape(TRACE_AT[-1], LANES),
            shape(len(KEPT), ROWS * SUB, LANES),
            shape(*FIELD),
            shape(*FIELD),
        ],
        in_specs=[VMEM] * 11,
        out_specs=[VMEM] * 5,
        scratch_shapes=[
            pltpu.VMEM(PADDED, jnp.float32),
            pltpu.VMEM(PADDED, jnp.float32),
            pltpu.VMEM((PLANES, OWN, CHUNKS * LANES), jnp.float32),
        ],
        compiler_params=pltpu.CompilerParams(vmem_limit_bytes=VMEM_LIMIT),
        name="first_pass",
    )(
        start_field, left_v, right_v, diffusivity, left_d, right_d, tiles, left_t, right_t,
        material, couple,
    )
    ends = lax.axis_size("zg") - 1
    from_below = lax.ppermute(to_above, "zg", [(i, i + 1) for i in range(ends)])
    from_above = lax.ppermute(to_below, "zg", [(i + 1, i) for i in range(ends)])
    return pl.pallas_call(
        second_kernel,
        out_shape=shape(*start_field.shape),
        in_specs=[VMEM] * 6,
        out_specs=VMEM,
        scratch_shapes=[pltpu.VMEM(PADDED, jnp.float32), pltpu.VMEM(PADDED, jnp.float32)],
        compiler_params=pltpu.CompilerParams(vmem_limit_bytes=VMEM_LIMIT),
        name="second_pass",
    )(from_below, from_above, kept, conduct, code, couple)


def solution(mesh):
    return jax.shard_map(
        on_device,
        mesh=mesh,
        in_specs=(P("zg", "xy", None), P("zg", "xy", None), P("zg", "xy", None), P(), P()),
        out_specs=P("zg", "xy", None),
        check_vma=False,
    )
```

```python
import jax
import jax.numpy as jnp
from jax import lax
from jax.experimental import pallas as pl
from jax.experimental.pallas import tpu as pltpu
from jax.sharding import PartitionSpec as P

TILE = 64
STEPS = 8
PLANES = 12
OWN = 8
HALO = 8
ROWS = OWN + 2 * HALO
SUB = 8
LANES = 128
CHUNKS = 8
VMEM_LIMIT = 24 * 1024 * 1024


SIDE = 4
OWN_AT = HALO * SUB
OWN_ROWS = OWN * SUB
HALF = SIDE * SUB
EDGE_PLANES = (0, 1, 2, 3, 8, 9, 10, 11)


def reach(level):
    margin = HALO - SIDE + 1 + level % SIDE
    return margin, ROWS - margin


def span(low, high):
    return pl.ds(low * SUB, (high - low) * SUB)


TRACE_AT = [0]
for _level in range(SIDE):
    _low, _high = reach(_level)
    TRACE_AT.append(TRACE_AT[-1] + (_high - _low) * SUB)


def trace_place(level):
    start = TRACE_AT[level % SIDE]
    return pl.ds(start, TRACE_AT[level % SIDE + 1] - start)


KEPT = [(level, plane) for level in range(6) for plane in sorted({level, level + 1, 10 - level, 11 - level})]
KEPT_AT = {pair: i for i, pair in enumerate(KEPT)}


def span_sum(cells):
    lane = lax.broadcasted_iota(jnp.int32, (1, SUB, LANES), 2)
    row = lax.broadcasted_iota(jnp.int32, (1, SUB, LANES), 1)
    first = lane == 0
    last = lane == LANES - 1
    corner = (first & (row == 0)) | (last & (row == SUB - 1))
    after = pltpu.roll(cells, LANES - 1, 2)
    before = pltpu.roll(cells, 1, 2)
    carry = jnp.where(last, pltpu.roll(after, SUB - 1, 1), pltpu.roll(before, 1, 1))
    carry = jnp.where(corner, 0.0, carry)
    return jnp.where(last, carry, after) + jnp.where(first, carry, before)


def split_cells(values):
    high = values.astype(jnp.bfloat16)
    low = (values - high.astype(jnp.float32)).astype(jnp.bfloat16)
    return high, low


def weights(couple_ref):
    high, low = split_cells(couple_ref[...])
    return jnp.concatenate([high, high, low], axis=0)


def advance(src, dst, conduct, code, weight, first, count, low, high):
    rows = high - low
    at = pl.ds(low * SUB, rows * SUB)
    mid = pl.ds(first + 1, count)
    here = src[mid, at, :]
    around = (
        src[pl.ds(first, count), at, :]
        + src[pl.ds(first + 2, count), at, :]
        + src[mid, pl.ds((low - 1) * SUB, rows * SUB), :]
        + src[mid, pl.ds((low + 1) * SUB, rows * SUB), :]
    )
    along = span_sum(here.reshape(count * rows, SUB, LANES)).reshape(here.shape)
    flat = here.reshape(count * rows * SUB, LANES)
    near, rest = split_cells(flat)
    product = jnp.dot(
        jnp.concatenate([near, rest, near], axis=1), weight, preferred_element_type=jnp.float32
    )
    plane = pl.ds(first, count)
    marks = code[plane, at, :]
    penalty = jnp.where(
        marks == 1.0,
        product[:, :LANES].reshape(here.shape),
        jnp.where(marks == 2.0, product[:, LANES:].reshape(here.shape), 0.0),
    )
    dst[mid, at, :] = here + conduct[plane, at, :] * (around + along - 6.0 * here) - penalty


def advance_groups(src, dst, conduct, code, weight, groups, count, stride, low, high):
    def body(i, carry):
        advance(src, dst, conduct, code, weight, i * stride, count, low, high)
        return carry

    if groups == 1:
        advance(src, dst, conduct, code, weight, 0, count, low, high)
    else:
        lax.fori_loop(0, groups, body, 0)


def spread(block, dst, offset, at_plane, planes=range(PLANES)):
    for plane in planes:
        for chunk in range(CHUNKS):
            dst[plane + at_plane, pl.ds(offset * SUB + chunk, OWN, stride=SUB), :] = block[
                plane, :, chunk * LANES : (chunk + 1) * LANES
            ]


def widened(codes):
    tile_of = lax.broadcasted_iota(jnp.int32, (LANES, CHUNKS * LANES), 0)
    cell_of = lax.broadcasted_iota(jnp.int32, (LANES, CHUNKS * LANES), 1)
    widen = jnp.where(tile_of == cell_of // TILE, 1.0, 0.0).astype(jnp.bfloat16)
    flat = codes.reshape(-1, LANES).astype(jnp.bfloat16)
    wide = jnp.dot(flat, widen, preferred_element_type=jnp.float32)
    return wide.reshape(codes.shape[0], OWN, CHUNKS * LANES)


def ghosts(src, low, high, from_below=None, from_above=None):
    at = span(low, high)
    if from_below is None:
        src[0, at, :] = src[1, at, :] * 0.6
        src[PLANES + 1, at, :] = src[PLANES, at, :] * 0.6
    else:
        src[0, at, :] = (from_below + 0.75 * src[1, at, :]) * 0.8
        src[PLANES + 1, at, :] = (from_above + 0.75 * src[PLANES, at, :]) * 0.8


def put_traces(src, to_below, to_above, level):
    at = span(*reach(level))
    place = trace_place(level)
    to_below[place, :] = 0.75 * src[2, at, :] - 0.25 * src[1, at, :]
    to_above[place, :] = 0.75 * src[PLANES - 1, at, :] - 0.25 * src[PLANES, at, :]


def prepare_kernel(
    own_v, own_d, own_t, material,
    near_right, near_left, far_right, far_left, field, conduct, code,
    tiles, wide,
):
    spread(own_v, field, 0, 0)
    spread(own_d, conduct, 0, 0)
    tiles[...] = jnp.zeros(tiles.shape, jnp.int32)
    tiles[:, :, : own_t.shape[2]] = own_t[...]
    table = material[...]
    row = lax.broadcasted_iota(jnp.int32, (SUB, LANES), 0)
    bits = jnp.zeros((SUB, LANES), jnp.int32)
    for part in range(table.shape[0] // SUB):
        bits = bits + (table[part * SUB : (part + 1) * SUB] << (row + part * SUB))
    for shift in (4, 2, 1):
        bits = bits + pltpu.roll(bits, shift, 0)
    parts = []
    for plane in range(PLANES):
        block = tiles[plane]
        entry = jnp.maximum(block - 1, 0)
        word = jnp.take_along_axis(bits, entry & (LANES - 1), axis=1)
        kind = (word >> (entry >> 7)) & 1
        codes = jnp.where(block > 0, kind + 1, 0).astype(jnp.float32)
        parts.append(codes[None])
        near_right[plane, 7 * SUB :, :] = codes
        near_left[plane, 7 * SUB :, :] = codes
    wide[...] = widened(jnp.concatenate(parts, axis=0))
    spread(wide, code, 0, 0)
    near_right[:, :HALF, :] = field[:, HALF:, :]
    near_right[:, HALF : 7 * SUB, :] = conduct[:, 5 * SUB :, :]
    near_left[:, :HALF, :] = field[:, :HALF, :]
    near_left[:, HALF : 7 * SUB, :] = conduct[:, : 3 * SUB, :]
    far_right[:, :HALF, :] = field[:, :HALF, :]
    far_right[:, HALF:, :] = conduct[:, SUB : 5 * SUB, :]
    far_left[:, :HALF, :] = field[:, HALF:, :]
    far_left[:, HALF:, :] = conduct[:, 3 * SUB : 7 * SUB, :]


def place_near(near_left, near_right, field, conduct, code, even, factor, marks, wide, planes):
    for plane in planes:
        even[plane + 1, pl.ds(OWN_AT, OWN_ROWS), :] = field[plane]
        even[plane + 1, pl.ds(4 * SUB, HALF), :] = near_left[plane, :HALF, :]
        even[plane + 1, pl.ds(16 * SUB, HALF), :] = near_right[plane, :HALF, :]
        factor[plane, pl.ds(OWN_AT, OWN_ROWS), :] = conduct[plane]
        factor[plane, pl.ds(5 * SUB, 3 * SUB), :] = near_left[plane, HALF : 7 * SUB, :]
        factor[plane, pl.ds(16 * SUB, 3 * SUB), :] = near_right[plane, HALF : 7 * SUB, :]
        marks[plane, pl.ds(OWN_AT, OWN_ROWS), :] = code[plane]
    for near, offset in ((near_left, 0), (near_right, HALO + OWN)):
        wide[...] = widened(near[:, 7 * SUB :, :])
        spread(wide, marks, offset, 0, planes)


def early_kernel(
    near_left, near_right, field, conduct, code, couple,
    to_below, to_above,
    even, odd, factor, marks, wide,
):
    weight = weights(couple)
    place_near(near_left, near_right, field, conduct, code, even, factor, marks, wide, EDGE_PLANES)
    for plane in (4, 7):
        even[plane + 1, pl.ds(OWN_AT, OWN_ROWS), :] = field[plane]
        even[plane + 1, pl.ds(4 * SUB, HALF), :] = near_left[plane, :HALF, :]
        even[plane + 1, pl.ds(16 * SUB, HALF), :] = near_right[plane, :HALF, :]
    buffers = (even, odd)
    for level in range(SIDE):
        src, dst = buffers[level % 2], buffers[1 - level % 2]
        put_traces(src, to_below, to_above, level)
        if level == SIDE - 1:
            break
        low, high = reach(level)
        ghosts(src, low, high)
        count = 4 - level
        advance_groups(src, dst, factor, marks, weight, 2, count, PLANES - count, low, high)


def first_kernel(
    near_left, near_right, far_left, far_right, field, conduct, code, couple,
    to_below, to_above, kept, factor, marks,
    even, odd, wide,
):
    weight = weights(couple)
    place_near(near_left, near_right, field, conduct, code, even, factor, marks, wide, range(PLANES))
    for plane in range(PLANES):
        even[plane + 1, pl.ds(0, HALF), :] = far_left[plane, :HALF, :]
        even[plane + 1, pl.ds(20 * SUB, HALF), :] = far_right[plane, :HALF, :]
        factor[plane, pl.ds(SUB, HALF), :] = far_left[plane, HALF:, :]
        factor[plane, pl.ds(19 * SUB, HALF), :] = far_right[plane, HALF:, :]
    buffers = (even, odd)
    for level in range(STEPS):
        src, dst = buffers[level % 2], buffers[1 - level % 2]
        if level >= SIDE:
            put_traces(src, to_below, to_above, level)
        inner_low, inner_high = reach(level)
        for plane in range(PLANES):
            if (level, plane) in KEPT_AT:
                at = span(inner_low - 1, inner_high + 1)
                kept[KEPT_AT[level, plane], at, :] = src[plane + 1, at, :]
        if level == STEPS - 1:
            break
        low, high = level + 1, ROWS - 1 - level
        if level >= 5:
            low, high = low + 1, high - 1
        ghosts(src, low, high)
        groups, count, stride = {5: (2, 3, 9), 6: (2, 2, 10)}.get(level, (3, 4, 4))
        advance_groups(src, dst, factor, marks, weight, groups, count, stride, low, high)


def second_steps(levels, buffers, kept, from_below, from_above, factor, marks, weight):
    for level in levels:
        src, dst = buffers[level % 2], buffers[1 - level % 2]
        low, high = reach(level)
        for plane in range(PLANES):
            if (level, plane) in KEPT_AT:
                at = span(low - 1, high + 1)
                src[plane + 1, at, :] = kept[KEPT_AT[level, plane], at, :]
        place = trace_place(level)
        ghosts(src, low, high, from_below[place, :], from_above[place, :])
        groups, count, stride = (2, level + 1, 11 - level) if level < 5 else (3, 4, 4)
        advance_groups(src, dst, factor, marks, weight, groups, count, stride, low, high)


def second_kernel(
    from_below, from_above, kept, factor, marks, couple,
    to_right, to_left, state,
    even, odd,
):
    second_steps(range(SIDE), (even, odd), kept, from_below, from_above, factor, marks, weights(couple))
    for i, plane in enumerate(EDGE_PLANES):
        state[i] = even[plane + 1, pl.ds(OWN_AT, OWN_ROWS), :]
        to_left[i] = even[plane + 1, pl.ds(OWN_AT, HALF), :]
        to_right[i] = even[plane + 1, pl.ds(OWN_AT + HALF, HALF), :]


def last_kernel(
    from_below, from_above, left, right, state, kept, factor, marks, couple,
    result,
    even, odd,
):
    for i, plane in enumerate(EDGE_PLANES):
        even[plane + 1, pl.ds(OWN_AT, OWN_ROWS), :] = state[i]
        even[plane + 1, pl.ds(OWN_AT - HALF, HALF), :] = left[i]
        even[plane + 1, pl.ds(OWN_AT + OWN_ROWS, HALF), :] = right[i]
    second_steps(
        range(SIDE, STEPS), (even, odd), kept, from_below, from_above, factor, marks, weights(couple)
    )
    for plane in range(PLANES):
        for chunk in range(CHUNKS):
            result[plane, :, chunk * LANES : (chunk + 1) * LANES] = even[
                plane + 1, pl.ds(OWN_AT + chunk, OWN, stride=SUB), :
            ]


def shape(*dims):
    return jax.ShapeDtypeStruct(dims, jnp.float32)


VMEM = pl.BlockSpec(memory_space=pltpu.VMEM)
FIELD = (PLANES, ROWS * SUB, LANES)
PADDED = (PLANES + 2, ROWS * SUB, LANES)
CELLS = (PLANES, OWN_ROWS, LANES)
TRACES = (TRACE_AT[-1], LANES)
WIDE = (PLANES, OWN, CHUNKS * LANES)
SHARE = (len(EDGE_PLANES), HALF, LANES)


def call(kernel, outs, scratch, *operands):
    return pl.pallas_call(
        kernel,
        out_shape=[shape(*dims) for dims in outs],
        in_specs=[VMEM] * len(operands),
        out_specs=[VMEM] * len(outs),
        scratch_shapes=scratch,
        compiler_params=pltpu.CompilerParams(vmem_limit_bytes=VMEM_LIMIT),
        name=kernel.__name__,
    )(*operands)


def scratch(*shapes):
    return [pltpu.VMEM(dims, jnp.float32) for dims in shapes]


def exchange(upward, downward, axis):
    ends = lax.axis_size(axis) - 1
    return (
        lax.ppermute(upward, axis, [(i, i + 1) for i in range(ends)]),
        lax.ppermute(downward, axis, [(i + 1, i) for i in range(ends)]),
    )


def on_device(start_field, diffusivity, tile_block, block_material, material_coupling):
    turned = jnp.swapaxes(material_coupling, 1, 2)
    empty = jnp.zeros((TILE, TILE), jnp.float32)
    couple = jnp.concatenate(
        [jnp.block([[turned[kind], empty], [empty, turned[kind]]]) for kind in (0, 1)], axis=1
    )
    near_right, near_left, far_right, far_left, field, conduct, code = call(
        prepare_kernel,
        [CELLS] * 7,
        [pltpu.VMEM((PLANES, OWN, LANES), jnp.int32)] + scratch(WIDE),
        start_field, diffusivity, tile_block, block_material.reshape(-1, LANES),
    )
    near = exchange(near_right, near_left, "xy")
    far = exchange(far_right, far_left, "xy")
    to_below, to_above = call(
        early_kernel, [TRACES] * 2, scratch(PADDED, PADDED, FIELD, FIELD, WIDE),
        *near, field, conduct, code, couple,
    )
    early = exchange(to_above, to_below, "zg")
    to_below, to_above, kept, factor, marks = call(
        first_kernel,
        [TRACES, TRACES, (len(KEPT), ROWS * SUB, LANES), FIELD, FIELD],
        scratch(PADDED, PADDED, WIDE),
        *near, *far, field, conduct, code, couple,
    )
    late = exchange(to_above, to_below, "zg")
    to_right, to_left, state = call(
        second_kernel,
        [SHARE, SHARE, (len(EDGE_PLANES), OWN_ROWS, LANES)],
        scratch(PADDED, PADDED),
        *early, kept, factor, marks, couple,
    )
    sides = exchange(to_right, to_left, "xy")
    (result,) = call(
        last_kernel,
        [start_field.shape],
        scratch(PADDED, PADDED),
        *late, *sides, state, kept, factor, marks, couple,
    )
    return result


def solution(mesh):
    return jax.shard_map(
        on_device,
        mesh=mesh,
        in_specs=(P("zg", "xy", None), P("zg", "xy", None), P("zg", "xy", None), P(), P()),
        out_specs=P("zg", "xy", None),
        check_vma=False,
    )
```

```python
import jax
import jax.numpy as jnp
from jax import lax
from jax.experimental import pallas as pl
from jax.experimental.pallas import tpu as pltpu
from jax.sharding import PartitionSpec as P

TILE = 64
STEPS = 8
PLANES = 12
OWN = 8
HALO = 8
ROWS = OWN + 2 * HALO
SUB = 8
LANES = 128
CHUNKS = 8
VMEM_LIMIT = 24 * 1024 * 1024


SIDE = 4
OWN_AT = HALO * SUB
OWN_ROWS = OWN * SUB
HALF = SIDE * SUB
EDGE_PLANES = (0, 1, 2, 3, 8, 9, 10, 11)


def reach(level):
    margin = HALO - SIDE + 1 + level % SIDE
    return margin, ROWS - margin


def span(low, high):
    return pl.ds(low * SUB, (high - low) * SUB)


TRACE_AT = [0]
for _level in range(SIDE):
    _low, _high = reach(_level)
    TRACE_AT.append(TRACE_AT[-1] + (_high - _low) * SUB)


def trace_place(level):
    start = TRACE_AT[level % SIDE]
    return pl.ds(start, TRACE_AT[level % SIDE + 1] - start)


KEPT = [(level, plane) for level in range(6) for plane in sorted({level, level + 1, 10 - level, 11 - level})]
KEPT_AT = {pair: i for i, pair in enumerate(KEPT)}


def span_sum(cells):
    lane = lax.broadcasted_iota(jnp.int32, (1, SUB, LANES), 2)
    row = lax.broadcasted_iota(jnp.int32, (1, SUB, LANES), 1)
    first = lane == 0
    last = lane == LANES - 1
    corner = (first & (row == 0)) | (last & (row == SUB - 1))
    after = pltpu.roll(cells, LANES - 1, 2)
    before = pltpu.roll(cells, 1, 2)
    carry = jnp.where(last, pltpu.roll(after, SUB - 1, 1), pltpu.roll(before, 1, 1))
    carry = jnp.where(corner, 0.0, carry)
    return jnp.where(last, carry, after) + jnp.where(first, carry, before)


def split_cells(values):
    high = values.astype(jnp.bfloat16)
    low = (values - high.astype(jnp.float32)).astype(jnp.bfloat16)
    return high, low


def weights(couple_ref):
    high, low = split_cells(couple_ref[...])
    return jnp.concatenate([high, high, low], axis=0)


def advance(src, dst, conduct, code, weight, first, count, low, high):
    rows = high - low
    at = pl.ds(low * SUB, rows * SUB)
    mid = pl.ds(first + 1, count)
    here = src[mid, at, :]
    around = (
        src[pl.ds(first, count), at, :]
        + src[pl.ds(first + 2, count), at, :]
        + src[mid, pl.ds((low - 1) * SUB, rows * SUB), :]
        + src[mid, pl.ds((low + 1) * SUB, rows * SUB), :]
    )
    along = span_sum(here.reshape(count * rows, SUB, LANES)).reshape(here.shape)
    flat = here.reshape(count * rows * SUB, LANES)
    near, rest = split_cells(flat)
    product = jnp.dot(
        jnp.concatenate([near, rest, near], axis=1), weight, preferred_element_type=jnp.float32
    )
    plane = pl.ds(first, count)
    marks = code[plane, at, :]
    penalty = jnp.where(
        marks == 1.0,
        product[:, :LANES].reshape(here.shape),
        jnp.where(marks == 2.0, product[:, LANES:].reshape(here.shape), 0.0),
    )
    dst[mid, at, :] = here + conduct[plane, at, :] * (around + along - 6.0 * here) - penalty


def advance_groups(src, dst, conduct, code, weight, groups, count, stride, low, high):
    def body(i, carry):
        advance(src, dst, conduct, code, weight, i * stride, count, low, high)
        return carry

    if groups == 1:
        advance(src, dst, conduct, code, weight, 0, count, low, high)
    else:
        lax.fori_loop(0, groups, body, 0)


def inside(axis):
    place = lax.axis_index(axis)
    return place > 0, place < lax.axis_size(axis) - 1


def kept_if(flag, values):
    return jnp.where(flag, values, 0.0)


def spread(block, dst, offset, at_plane, planes=range(PLANES)):
    for plane in planes:
        for chunk in range(CHUNKS):
            dst[plane + at_plane, pl.ds(offset * SUB + chunk, OWN, stride=SUB), :] = block[
                plane, :, chunk * LANES : (chunk + 1) * LANES
            ]


def widened(codes):
    tile_of = lax.broadcasted_iota(jnp.int32, (LANES, CHUNKS * LANES), 0)
    cell_of = lax.broadcasted_iota(jnp.int32, (LANES, CHUNKS * LANES), 1)
    widen = jnp.where(tile_of == cell_of // TILE, 1.0, 0.0).astype(jnp.bfloat16)
    flat = codes.reshape(-1, LANES).astype(jnp.bfloat16)
    wide = jnp.dot(flat, widen, preferred_element_type=jnp.float32)
    return wide.reshape(codes.shape[0], OWN, CHUNKS * LANES)


def ghosts(src, low, high, from_below=None, from_above=None):
    at = span(low, high)
    if from_below is None:
        src[0, at, :] = src[1, at, :] * 0.6
        src[PLANES + 1, at, :] = src[PLANES, at, :] * 0.6
    else:
        src[0, at, :] = (from_below + 0.75 * src[1, at, :]) * 0.8
        src[PLANES + 1, at, :] = (from_above + 0.75 * src[PLANES, at, :]) * 0.8


def put_traces(src, to_below, to_above, level):
    at = span(*reach(level))
    place = trace_place(level)
    to_below[place, :] = 0.75 * src[2, at, :] - 0.25 * src[1, at, :]
    to_above[place, :] = 0.75 * src[PLANES - 1, at, :] - 0.25 * src[PLANES, at, :]


def prepare_kernel(
    start_field, diffusivity, tile_block, block_material,
    near_right, near_left, far_right, far_left, field, conduct, code,
    own_v, own_d, own_t, material, tiles, wide, arrived,
):
    copies = [
        pltpu.make_async_copy(source, target, arrived.at[i])
        for i, (source, target) in enumerate(
            ((start_field, own_v), (diffusivity, own_d), (tile_block, own_t), (block_material, material))
        )
    ]
    for copy in copies:
        copy.start()
    copies[0].wait()
    spread(own_v, field, 0, 0)
    copies[1].wait()
    spread(own_d, conduct, 0, 0)
    copies[2].wait()
    copies[3].wait()
    tiles[...] = jnp.zeros(tiles.shape, jnp.int32)
    tiles[:, :, : own_t.shape[2]] = own_t[...]
    table = material[...]
    row = lax.broadcasted_iota(jnp.int32, (SUB, LANES), 0)
    bits = jnp.zeros((SUB, LANES), jnp.int32)
    for part in range(table.shape[0] // SUB):
        bits = bits + (table[part * SUB : (part + 1) * SUB] << (row + part * SUB))
    for shift in (4, 2, 1):
        bits = bits + pltpu.roll(bits, shift, 0)
    parts = []
    for plane in range(PLANES):
        block = tiles[plane]
        entry = jnp.maximum(block - 1, 0)
        word = jnp.take_along_axis(bits, entry & (LANES - 1), axis=1)
        kind = (word >> (entry >> 7)) & 1
        codes = jnp.where(block > 0, kind + 1, 0).astype(jnp.float32)
        parts.append(codes[None])
        near_right[plane, 7 * SUB :, :] = codes
        near_left[plane, 7 * SUB :, :] = codes
    wide[...] = widened(jnp.concatenate(parts, axis=0))
    spread(wide, code, 0, 0)
    near_right[:, :HALF, :] = field[:, HALF:, :]
    near_right[:, HALF : 7 * SUB, :] = conduct[:, 5 * SUB :, :]
    near_left[:, :HALF, :] = field[:, :HALF, :]
    near_left[:, HALF : 7 * SUB, :] = conduct[:, : 3 * SUB, :]
    far_right[:, :HALF, :] = field[:, :HALF, :]
    far_right[:, HALF:, :] = conduct[:, SUB : 5 * SUB, :]
    far_left[:, :HALF, :] = field[:, HALF:, :]
    far_left[:, HALF:, :] = conduct[:, 3 * SUB : 7 * SUB, :]


def place_field(near_left, near_right, field, even, plane):
    has_left, has_right = inside("xy")
    even[plane + 1, pl.ds(OWN_AT, OWN_ROWS), :] = field[plane]
    even[plane + 1, pl.ds(4 * SUB, HALF), :] = kept_if(has_left, near_left[plane, :HALF, :])
    even[plane + 1, pl.ds(16 * SUB, HALF), :] = kept_if(has_right, near_right[plane, :HALF, :])


def place_near(near_left, near_right, field, conduct, code, even, factor, marks, wide, planes):
    has_left, has_right = inside("xy")
    for plane in planes:
        place_field(near_left, near_right, field, even, plane)
        factor[plane, pl.ds(OWN_AT, OWN_ROWS), :] = conduct[plane]
        factor[plane, pl.ds(5 * SUB, 3 * SUB), :] = kept_if(has_left, near_left[plane, HALF : 7 * SUB, :])
        factor[plane, pl.ds(16 * SUB, 3 * SUB), :] = kept_if(has_right, near_right[plane, HALF : 7 * SUB, :])
        marks[plane, pl.ds(OWN_AT, OWN_ROWS), :] = code[plane]
    for flag, near, offset in ((has_left, near_left, 0), (has_right, near_right, HALO + OWN)):
        wide[...] = widened(kept_if(flag, near[:, 7 * SUB :, :]))
        spread(wide, marks, offset, 0, planes)


def early_kernel(
    near_left, near_right, field, conduct, code, couple,
    to_below, to_above,
    even, odd, factor, marks, wide,
):
    weight = weights(couple)
    place_near(near_left, near_right, field, conduct, code, even, factor, marks, wide, EDGE_PLANES)
    for plane in (4, 7):
        place_field(near_left, near_right, field, even, plane)
    buffers = (even, odd)
    for level in range(SIDE):
        src, dst = buffers[level % 2], buffers[1 - level % 2]
        put_traces(src, to_below, to_above, level)
        if level == SIDE - 1:
            break
        low, high = reach(level)
        ghosts(src, low, high)
        count = 4 - level
        advance_groups(src, dst, factor, marks, weight, 2, count, PLANES - count, low, high)


def first_kernel(
    near_left, near_right, far_left, far_right, field, conduct, code, couple,
    to_below, to_above, kept, factor, marks,
    even, odd, wide,
):
    weight = weights(couple)
    place_near(near_left, near_right, field, conduct, code, even, factor, marks, wide, range(PLANES))
    has_left, has_right = inside("xy")
    for plane in range(PLANES):
        even[plane + 1, pl.ds(0, HALF), :] = kept_if(has_left, far_left[plane, :HALF, :])
        even[plane + 1, pl.ds(20 * SUB, HALF), :] = kept_if(has_right, far_right[plane, :HALF, :])
        factor[plane, pl.ds(SUB, HALF), :] = kept_if(has_left, far_left[plane, HALF:, :])
        factor[plane, pl.ds(19 * SUB, HALF), :] = kept_if(has_right, far_right[plane, HALF:, :])
    buffers = (even, odd)
    for level in range(STEPS):
        src, dst = buffers[level % 2], buffers[1 - level % 2]
        if level >= SIDE:
            put_traces(src, to_below, to_above, level)
        inner_low, inner_high = reach(level)
        for plane in range(PLANES):
            if (level, plane) in KEPT_AT:
                at = span(inner_low - 1, inner_high + 1)
                kept[KEPT_AT[level, plane], at, :] = src[plane + 1, at, :]
        if level == STEPS - 1:
            break
        low, high = level + 1, ROWS - 1 - level
        if level >= 5:
            low, high = low + 1, high - 1
        ghosts(src, low, high)
        groups, count, stride = {5: (2, 3, 9), 6: (2, 2, 10)}.get(level, (3, 4, 4))
        advance_groups(src, dst, factor, marks, weight, groups, count, stride, low, high)


def second_steps(levels, buffers, kept, from_below, from_above, factor, marks, weight):
    has_below, has_above = inside("zg")
    for level in levels:
        src, dst = buffers[level % 2], buffers[1 - level % 2]
        low, high = reach(level)
        for plane in range(PLANES):
            if (level, plane) in KEPT_AT:
                at = span(low - 1, high + 1)
                src[plane + 1, at, :] = kept[KEPT_AT[level, plane], at, :]
        place = trace_place(level)
        ghosts(
            src, low, high,
            kept_if(has_below, from_below[place, :]), kept_if(has_above, from_above[place, :]),
        )
        groups, count, stride = (2, level + 1, 11 - level) if level < 5 else (3, 4, 4)
        advance_groups(src, dst, factor, marks, weight, groups, count, stride, low, high)


def second_kernel(
    from_below, from_above, kept, factor, marks, couple,
    to_right, to_left, state,
    even, odd,
):
    second_steps(range(SIDE), (even, odd), kept, from_below, from_above, factor, marks, weights(couple))
    for i, plane in enumerate(EDGE_PLANES):
        state[i] = even[plane + 1, pl.ds(OWN_AT, OWN_ROWS), :]
        to_left[i] = even[plane + 1, pl.ds(OWN_AT, HALF), :]
        to_right[i] = even[plane + 1, pl.ds(OWN_AT + HALF, HALF), :]


def last_kernel(
    from_below, from_above, left, right, state, kept, factor, marks, couple,
    result,
    even, odd,
):
    has_left, has_right = inside("xy")
    for i, plane in enumerate(EDGE_PLANES):
        even[plane + 1, pl.ds(OWN_AT, OWN_ROWS), :] = state[i]
        even[plane + 1, pl.ds(OWN_AT - HALF, HALF), :] = kept_if(has_left, left[i])
        even[plane + 1, pl.ds(OWN_AT + OWN_ROWS, HALF), :] = kept_if(has_right, right[i])
    second_steps(
        range(SIDE, STEPS), (even, odd), kept, from_below, from_above, factor, marks, weights(couple)
    )
    for plane in range(PLANES):
        for chunk in range(CHUNKS):
            result[plane, :, chunk * LANES : (chunk + 1) * LANES] = even[
                plane + 1, pl.ds(OWN_AT + chunk, OWN, stride=SUB), :
            ]


def shape(*dims):
    return jax.ShapeDtypeStruct(dims, jnp.float32)


VMEM = pl.BlockSpec(memory_space=pltpu.VMEM)
FIELD = (PLANES, ROWS * SUB, LANES)
PADDED = (PLANES + 2, ROWS * SUB, LANES)
CELLS = (PLANES, OWN_ROWS, LANES)
TRACES = (TRACE_AT[-1], LANES)
WIDE = (PLANES, OWN, CHUNKS * LANES)
SHARE = (len(EDGE_PLANES), HALF, LANES)


def call(kernel, outs, scratch, *operands, place=VMEM):
    return pl.pallas_call(
        kernel,
        out_shape=[shape(*dims) for dims in outs],
        in_specs=[place] * len(operands),
        out_specs=[VMEM] * len(outs),
        scratch_shapes=scratch,
        compiler_params=pltpu.CompilerParams(vmem_limit_bytes=VMEM_LIMIT),
        name=kernel.__name__,
    )(*operands)


def scratch(*shapes):
    return [pltpu.VMEM(dims, jnp.float32) for dims in shapes]


def exchange(upward, downward, axis):
    count = lax.axis_size(axis)
    return (
        lax.ppermute(upward, axis, [(i, (i + 1) % count) for i in range(count)]),
        lax.ppermute(downward, axis, [((i + 1) % count, i) for i in range(count)]),
    )


def on_device(start_field, diffusivity, tile_block, block_material, material_coupling):
    turned = jnp.swapaxes(material_coupling, 1, 2)
    empty = jnp.zeros((TILE, TILE), jnp.float32)
    couple = jnp.concatenate(
        [jnp.block([[turned[kind], empty], [empty, turned[kind]]]) for kind in (0, 1)], axis=1
    )
    material = block_material.reshape(-1, LANES)
    near_right, near_left, far_right, far_left, field, conduct, code = call(
        prepare_kernel,
        [CELLS] * 7,
        scratch(start_field.shape, diffusivity.shape)
        + [
            pltpu.VMEM(tile_block.shape, jnp.int32),
            pltpu.VMEM(material.shape, jnp.int32),
            pltpu.VMEM((PLANES, OWN, LANES), jnp.int32),
        ]
        + scratch(WIDE)
        + [pltpu.SemaphoreType.DMA((4,))],
        start_field, diffusivity, tile_block, material,
        place=pl.BlockSpec(memory_space=pltpu.HBM),
    )
    near = exchange(near_right, near_left, "xy")
    far = exchange(far_right, far_left, "xy")
    to_below, to_above = call(
        early_kernel, [TRACES] * 2, scratch(PADDED, PADDED, FIELD, FIELD, WIDE),
        *near, field, conduct, code, couple,
    )
    early = exchange(to_above, to_below, "zg")
    to_below, to_above, kept, factor, marks = call(
        first_kernel,
        [TRACES, TRACES, (len(KEPT), ROWS * SUB, LANES), FIELD, FIELD],
        scratch(PADDED, PADDED, WIDE),
        *near, *far, field, conduct, code, couple,
    )
    late = exchange(to_above, to_below, "zg")
    to_right, to_left, state = call(
        second_kernel,
        [SHARE, SHARE, (len(EDGE_PLANES), OWN_ROWS, LANES)],
        scratch(PADDED, PADDED),
        *early, kept, factor, marks, couple,
    )
    sides = exchange(to_right, to_left, "xy")
    (result,) = call(
        last_kernel,
        [start_field.shape],
        scratch(PADDED, PADDED),
        *late, *sides, state, kept, factor, marks, couple,
    )
    return result


def solution(mesh):
    return jax.shard_map(
        on_device,
        mesh=mesh,
        in_specs=(P("zg", "xy", None), P("zg", "xy", None), P("zg", "xy", None), P(), P()),
        out_specs=P("zg", "xy", None),
        check_vma=False,
    )
```

```python
import jax
import jax.numpy as jnp
from jax import lax
from jax.experimental import pallas as pl
from jax.experimental.pallas import tpu as pltpu
from jax.sharding import PartitionSpec as P

TILE = 64
STEPS = 8
PLANES = 12
OWN = 8
HALO = 8
ROWS = OWN + 2 * HALO
SUB = 8
LANES = 128
CHUNKS = 8
VMEM_LIMIT = 24 * 1024 * 1024


SIDE = 4
OWN_AT = HALO * SUB
OWN_ROWS = OWN * SUB
HALF = SIDE * SUB
EDGE_PLANES = (0, 1, 2, 3, 8, 9, 10, 11)
INNER_PLANES = (4, 5, 6, 7)
REST = 3 * SUB
NEAR = HALF + REST
CODES_AT = PLANES * NEAR
INNER_AT = len(EDGE_PLANES) * REST


def reach(level):
    margin = HALO - SIDE + 1 + level % SIDE
    return margin, ROWS - margin


def span(low, high):
    return pl.ds(low * SUB, (high - low) * SUB)


TRACE_AT = [0]
for _level in range(SIDE):
    _low, _high = reach(_level)
    TRACE_AT.append(TRACE_AT[-1] + (_high - _low) * SUB)


def trace_place(level):
    start = TRACE_AT[level % SIDE]
    return pl.ds(start, TRACE_AT[level % SIDE + 1] - start)


KEPT = [(level, plane) for level in range(6) for plane in sorted({level, level + 1, 10 - level, 11 - level})]
EARLY_KEPT = {pair: i for i, pair in enumerate(pair for pair in KEPT if pair[0] < SIDE)}
LATE_KEPT = {pair: i for i, pair in enumerate(pair for pair in KEPT if pair[0] >= SIDE)}


def span_sum(cells):
    lane = lax.broadcasted_iota(jnp.int32, (1, SUB, LANES), 2)
    row = lax.broadcasted_iota(jnp.int32, (1, SUB, LANES), 1)
    first = lane == 0
    last = lane == LANES - 1
    corner = (first & (row == 0)) | (last & (row == SUB - 1))
    after = pltpu.roll(cells, LANES - 1, 2)
    before = pltpu.roll(cells, 1, 2)
    carry = jnp.where(last, pltpu.roll(after, SUB - 1, 1), pltpu.roll(before, 1, 1))
    carry = jnp.where(corner, 0.0, carry)
    return jnp.where(last, carry, after) + jnp.where(first, carry, before)


def split_cells(values):
    high = values.astype(jnp.bfloat16)
    low = (values - high.astype(jnp.float32)).astype(jnp.bfloat16)
    return high, low


def weights(couple_ref):
    high, low = split_cells(couple_ref[...])
    return jnp.concatenate([high, high, low], axis=0)


def advance(src, dst, conduct, code, weight, first, count, low, high):
    rows = high - low
    at = pl.ds(low * SUB, rows * SUB)
    mid = pl.ds(first + 1, count)
    here = src[mid, at, :]
    around = (
        src[pl.ds(first, count), at, :]
        + src[pl.ds(first + 2, count), at, :]
        + src[mid, pl.ds((low - 1) * SUB, rows * SUB), :]
        + src[mid, pl.ds((low + 1) * SUB, rows * SUB), :]
    )
    along = span_sum(here.reshape(count * rows, SUB, LANES)).reshape(here.shape)
    flat = here.reshape(count * rows * SUB, LANES)
    near, rest = split_cells(flat)
    product = jnp.dot(
        jnp.concatenate([near, rest, near], axis=1), weight, preferred_element_type=jnp.float32
    )
    plane = pl.ds(first, count)
    marks = code[plane, at, :]
    penalty = jnp.where(
        marks == 1.0,
        product[:, :LANES].reshape(here.shape),
        jnp.where(marks == 2.0, product[:, LANES:].reshape(here.shape), 0.0),
    )
    dst[mid, at, :] = here + conduct[plane, at, :] * (around + along - 6.0 * here) - penalty


def advance_groups(src, dst, conduct, code, weight, groups, count, stride, low, high):
    for i in range(groups):
        advance(src, dst, conduct, code, weight, i * stride, count, low, high)


def inside(axis):
    place = lax.axis_index(axis)
    return place > 0, place < lax.axis_size(axis) - 1


def kept_if(flag, values):
    return jnp.where(flag, values, 0.0)


def spread(block, dst, offset, at_plane, planes=range(PLANES)):
    for plane in planes:
        for chunk in range(CHUNKS):
            dst[plane + at_plane, pl.ds(offset * SUB + chunk, OWN, stride=SUB), :] = block[
                plane, :, chunk * LANES : (chunk + 1) * LANES
            ]


def widened(codes):
    tile_of = lax.broadcasted_iota(jnp.int32, (LANES, CHUNKS * LANES), 0)
    cell_of = lax.broadcasted_iota(jnp.int32, (LANES, CHUNKS * LANES), 1)
    widen = jnp.where(tile_of == cell_of // TILE, 1.0, 0.0).astype(jnp.bfloat16)
    flat = codes.reshape(-1, LANES).astype(jnp.bfloat16)
    wide = jnp.dot(flat, widen, preferred_element_type=jnp.float32)
    return wide.reshape(codes.shape[0], OWN, CHUNKS * LANES)


def ghosts(src, low, high, from_below=None, from_above=None):
    at = span(low, high)
    if from_below is None:
        src[0, at, :] = src[1, at, :] * 0.6
        src[PLANES + 1, at, :] = src[PLANES, at, :] * 0.6
    else:
        src[0, at, :] = (from_below + 0.75 * src[1, at, :]) * 0.8
        src[PLANES + 1, at, :] = (from_above + 0.75 * src[PLANES, at, :]) * 0.8


def put_traces(src, to_below, to_above, level):
    at = span(*reach(level))
    place = trace_place(level)
    to_below[place, :] = 0.75 * src[2, at, :] - 0.25 * src[1, at, :]
    to_above[place, :] = 0.75 * src[PLANES - 1, at, :] - 0.25 * src[PLANES, at, :]


def prepare_kernel(
    start_field, diffusivity, tile_block, block_material,
    to_right, to_left, code,
    own_v, own_d, own_t, material, tiles, field, conduct, arrived,
):
    copies = [
        pltpu.make_async_copy(source, target, arrived.at[i])
        for i, (source, target) in enumerate(
            ((start_field, own_v), (diffusivity, own_d), (tile_block, own_t), (block_material, material))
        )
    ]
    for copy in copies:
        copy.start()
    copies[0].wait()
    spread(own_v, field, 0, 0)
    copies[1].wait()
    spread(own_d, conduct, 0, 0)
    copies[2].wait()
    copies[3].wait()
    tiles[...] = jnp.zeros(tiles.shape, jnp.int32)
    tiles[:, :, : own_t.shape[2]] = own_t[...]
    table = material[...]
    row = lax.broadcasted_iota(jnp.int32, (SUB, LANES), 0)
    bits = jnp.zeros((SUB, LANES), jnp.int32)
    for part in range(table.shape[0] // SUB):
        bits = bits + (table[part * SUB : (part + 1) * SUB] << (row + part * SUB))
    for shift in (4, 2, 1):
        bits = bits + pltpu.roll(bits, shift, 0)
    for plane in range(PLANES):
        block = tiles[plane]
        entry = jnp.maximum(block - 1, 0)
        word = jnp.take_along_axis(bits, entry & (LANES - 1), axis=1)
        kind = (word >> (entry >> 7)) & 1
        code[plane] = jnp.where(block > 0, kind + 1, 0).astype(jnp.float32)
        at = plane * NEAR
        to_right[at : at + HALF, :] = field[plane, HALF:, :]
        to_right[at + HALF : at + NEAR, :] = conduct[plane, OWN_ROWS - REST :, :]
        to_left[at : at + HALF, :] = field[plane, :HALF, :]
        to_left[at + HALF : at + NEAR, :] = conduct[plane, :REST, :]
        at = CODES_AT + 3 * plane
        to_right[at : at + 3, :] = code[plane, 5:, :]
        to_left[at : at + 3, :] = code[plane, :3, :]
    to_right[CODES_AT + 3 * PLANES :, :] = jnp.zeros((4, LANES), jnp.float32)
    to_left[CODES_AT + 3 * PLANES :, :] = jnp.zeros((4, LANES), jnp.float32)


def own_kernel(start_field, diffusivity, code, even, factor, marks, wide):
    spread(start_field, even, HALO, 0)
    spread(diffusivity, factor, HALO, 0)
    wide[...] = widened(code[...])
    spread(wide, marks, HALO, 0)


def keep(src, kept, places, level):
    low, high = reach(level)
    at = span(low - 1, high + 1)
    for plane in range(PLANES):
        if (level, plane) in places:
            kept[places[level, plane], at, :] = src[plane + 1, at, :]


def first_kernel(
    left, right, field, conduct, code, couple,
    to_right, to_left, to_below, to_above, state, kept, factor, marks,
    even, odd, wide, codes,
):
    weight = weights(couple)
    has_left, has_right = inside("xy")
    own = pl.ds(OWN_AT, OWN_ROWS)
    for flag, packet, offset, near_at, rest_at, first in (
        (has_left, left, 0, 4 * SUB, 5 * SUB, 5),
        (has_right, right, HALO + OWN, 16 * SUB, 16 * SUB, 0),
    ):
        codes[...] = jnp.zeros(codes.shape, jnp.float32)
        for plane in range(PLANES):
            at = plane * NEAR
            even[plane + 1, pl.ds(near_at, HALF), :] = kept_if(flag, packet[at : at + HALF, :])
            factor[plane, pl.ds(rest_at, REST), :] = kept_if(flag, packet[at + HALF : at + NEAR, :])
            at = CODES_AT + 3 * plane
            codes[plane, first : first + 3, :] = kept_if(flag, packet[at : at + 3, :])
        wide[...] = widened(codes[...])
        spread(wide, marks, offset, 0)
    even[1 : PLANES + 1, own, :] = field[:, own, :]
    factor[:, own, :] = conduct[:, own, :]
    marks[:, own, :] = code[:, own, :]
    buffers = (even, odd)
    for level in range(SIDE):
        src, dst = buffers[level % 2], buffers[1 - level % 2]
        put_traces(src, to_below, to_above, level)
        keep(src, kept, EARLY_KEPT, level)
        low, high = reach(level)
        ghosts(src, low, high)
        advance_groups(src, dst, factor, marks, weight, 1, PLANES, 0, low, high)
    state[...] = even[1 : PLANES + 1, OWN_AT : OWN_AT + OWN_ROWS, :]
    for i, plane in enumerate(EDGE_PLANES):
        at = i * REST
        to_left[at : at + REST, :] = state[plane, :REST, :]
        to_right[at : at + REST, :] = state[plane, OWN_ROWS - REST :, :]
    for i, plane in enumerate(INNER_PLANES):
        at = INNER_AT + i * HALF
        to_left[at : at + HALF, :] = state[plane, :HALF, :]
        to_right[at : at + HALF, :] = state[plane, HALF:, :]


def middle_kernel(
    left, right, state, factor, marks, couple,
    to_below, to_above, kept,
    even, odd,
):
    weight = weights(couple)
    has_left, has_right = inside("xy")
    for plane in range(PLANES):
        even[plane + 1, pl.ds(OWN_AT, OWN_ROWS), :] = state[plane]
    for i, plane in enumerate(EDGE_PLANES):
        at = i * REST
        even[plane + 1, pl.ds(5 * SUB, REST), :] = kept_if(has_left, left[at : at + REST, :])
        even[plane + 1, pl.ds(16 * SUB, REST), :] = kept_if(has_right, right[at : at + REST, :])
    for i, plane in enumerate(INNER_PLANES):
        at = INNER_AT + i * HALF
        even[plane + 1, pl.ds(4 * SUB, HALF), :] = kept_if(has_left, left[at : at + HALF, :])
        even[plane + 1, pl.ds(16 * SUB, HALF), :] = kept_if(has_right, right[at : at + HALF, :])
    buffers = (even, odd)
    for level in range(SIDE, STEPS):
        src, dst = buffers[level % 2], buffers[1 - level % 2]
        put_traces(src, to_below, to_above, level)
        keep(src, kept, LATE_KEPT, level)
        if level == STEPS - 1:
            break
        low, high = reach(level)
        ghosts(src, low + 1, high - 1)
        count = STEPS - level
        advance_groups(src, dst, factor, marks, weight, 2, count, PLANES - count, low + 1, high - 1)
        if level == SIDE:
            advance(src, dst, factor, marks, weight, 5, 2, low, high)


def second_steps(levels, buffers, kept, places, from_below, from_above, factor, marks, weight):
    has_below, has_above = inside("zg")
    for level in levels:
        src, dst = buffers[level % 2], buffers[1 - level % 2]
        low, high = reach(level)
        for plane in range(PLANES):
            if (level, plane) in places:
                at = span(low - 1, high + 1)
                src[plane + 1, at, :] = kept[places[level, plane], at, :]
        place = trace_place(level)
        ghosts(
            src, low, high,
            kept_if(has_below, from_below[place, :]), kept_if(has_above, from_above[place, :]),
        )
        groups, count, stride = (2, level + 1, 11 - level) if level < 5 else (1, PLANES, 0)
        advance_groups(src, dst, factor, marks, weight, groups, count, stride, low, high)


def second_kernel(
    from_below, from_above, kept, factor, marks, couple,
    to_right, to_left, state,
    even, odd,
):
    second_steps(range(SIDE), (even, odd), kept, EARLY_KEPT, from_below, from_above, factor, marks, weights(couple))
    for i, plane in enumerate(EDGE_PLANES):
        state[i] = even[plane + 1, pl.ds(OWN_AT, OWN_ROWS), :]
        to_left[i] = even[plane + 1, pl.ds(OWN_AT, HALF), :]
        to_right[i] = even[plane + 1, pl.ds(OWN_AT + HALF, HALF), :]


def last_kernel(
    from_below, from_above, left, right, state, kept, factor, marks, couple,
    result,
    even, odd,
):
    has_left, has_right = inside("xy")
    for i, plane in enumerate(EDGE_PLANES):
        even[plane + 1, pl.ds(OWN_AT, OWN_ROWS), :] = state[i]
        even[plane + 1, pl.ds(OWN_AT - HALF, HALF), :] = kept_if(has_left, left[i])
        even[plane + 1, pl.ds(OWN_AT + OWN_ROWS, HALF), :] = kept_if(has_right, right[i])
    second_steps(
        range(SIDE, STEPS), (even, odd), kept, LATE_KEPT, from_below, from_above, factor, marks,
        weights(couple),
    )
    for plane in range(PLANES):
        for chunk in range(CHUNKS):
            result[plane, :, chunk * LANES : (chunk + 1) * LANES] = even[
                plane + 1, pl.ds(OWN_AT + chunk, OWN, stride=SUB), :
            ]


def shape(*dims):
    return jax.ShapeDtypeStruct(dims, jnp.float32)


VMEM = pl.BlockSpec(memory_space=pltpu.VMEM)
FIELD = (PLANES, ROWS * SUB, LANES)
PADDED = (PLANES + 2, ROWS * SUB, LANES)
CELLS = (PLANES, OWN_ROWS, LANES)
TRACES = (TRACE_AT[-1], LANES)
WIDE = (PLANES, OWN, CHUNKS * LANES)
PACKET = (CODES_AT + 3 * PLANES + 4, LANES)
SHARE = (INNER_AT + len(INNER_PLANES) * HALF, LANES)
EDGE_SHARE = (len(EDGE_PLANES), HALF, LANES)


def call(kernel, outs, scratch, *operands, place=VMEM, limit=VMEM_LIMIT):
    return pl.pallas_call(
        kernel,
        out_shape=[shape(*dims) for dims in outs],
        in_specs=[place] * len(operands),
        out_specs=[VMEM] * len(outs),
        scratch_shapes=scratch,
        compiler_params=pltpu.CompilerParams(vmem_limit_bytes=limit),
        name=kernel.__name__,
    )(*operands)


def scratch(*shapes):
    return [pltpu.VMEM(dims, jnp.float32) for dims in shapes]


def exchange(upward, downward, axis):
    count = lax.axis_size(axis)
    return (
        lax.ppermute(upward, axis, [(i, (i + 1) % count) for i in range(count)]),
        lax.ppermute(downward, axis, [((i + 1) % count, i) for i in range(count)]),
    )


def on_device(start_field, diffusivity, tile_block, block_material, material_coupling):
    turned = jnp.swapaxes(material_coupling, 1, 2)
    empty = jnp.zeros((TILE, TILE), jnp.float32)
    couple = jnp.concatenate(
        [jnp.block([[turned[kind], empty], [empty, turned[kind]]]) for kind in (0, 1)], axis=1
    )
    material = block_material.reshape(-1, LANES)
    to_right, to_left, code = call(
        prepare_kernel,
        [PACKET, PACKET, (PLANES, OWN, LANES)],
        scratch(start_field.shape, diffusivity.shape)
        + [
            pltpu.VMEM(tile_block.shape, jnp.int32),
            pltpu.VMEM(material.shape, jnp.int32),
            pltpu.VMEM((PLANES, OWN, LANES), jnp.int32),
        ]
        + scratch(CELLS, CELLS)
        + [pltpu.SemaphoreType.DMA((4,))],
        start_field, diffusivity, tile_block, material,
        place=pl.BlockSpec(memory_space=pltpu.HBM),
        limit=56 * 1024 * 1024,
    )
    near = exchange(to_right, to_left, "xy")
    field, conduct, code = call(
        own_kernel, [FIELD] * 3, scratch(WIDE), start_field, diffusivity, code
    )
    to_right, to_left, to_below, to_above, state, early_kept, factor, marks = call(
        first_kernel,
        [SHARE, SHARE, TRACES, TRACES, CELLS, (len(EARLY_KEPT), ROWS * SUB, LANES), FIELD, FIELD],
        scratch(PADDED, PADDED, WIDE, (PLANES, OWN, LANES)),
        *near, field, conduct, code, couple,
    )
    sides = exchange(to_right, to_left, "xy")
    early = exchange(to_above, to_below, "zg")
    to_below, to_above, late_kept = call(
        middle_kernel,
        [TRACES, TRACES, (len(LATE_KEPT), ROWS * SUB, LANES)],
        scratch(PADDED, PADDED),
        *sides, state, factor, marks, couple,
    )
    late = exchange(to_above, to_below, "zg")
    to_right, to_left, state = call(
        second_kernel,
        [EDGE_SHARE, EDGE_SHARE, (len(EDGE_PLANES), OWN_ROWS, LANES)],
        scratch(PADDED, PADDED),
        *early, early_kept, factor, marks, couple,
    )
    sides = exchange(to_right, to_left, "xy")
    (result,) = call(
        last_kernel,
        [start_field.shape],
        scratch(PADDED, PADDED),
        *late, *sides, state, late_kept, factor, marks, couple,
    )
    return result


def solution(mesh):
    return jax.shard_map(
        on_device,
        mesh=mesh,
        in_specs=(P("zg", "xy", None), P("zg", "xy", None), P("zg", "xy", None), P(), P()),
        out_specs=P("zg", "xy", None),
        check_vma=False,
    )
```

```python
import jax
import jax.numpy as jnp
from jax import lax
from jax.experimental import pallas as pl
from jax.experimental.pallas import tpu as pltpu
from jax.sharding import PartitionSpec as P

TILE = 64
STEPS = 8
PLANES = 12
OWN = 8
HALO = 8
ROWS = OWN + 2 * HALO
SUB = 8
LANES = 128
CHUNKS = 8
VMEM_LIMIT = 24 * 1024 * 1024


SIDE = 4
OWN_AT = HALO * SUB
OWN_ROWS = OWN * SUB
HALF = SIDE * SUB
EDGE_PLANES = (0, 1, 2, 3, 8, 9, 10, 11)
INNER_PLANES = (4, 5, 6, 7)
REST = 3 * SUB
NEAR = HALF + REST
CODES_AT = PLANES * NEAR
INNER_AT = len(EDGE_PLANES) * REST


def reach(level):
    margin = HALO - SIDE + 1 + level % SIDE
    return margin, ROWS - margin


def span(low, high):
    return pl.ds(low * SUB, (high - low) * SUB)


TRACE_AT = [0]
for _level in range(SIDE):
    _low, _high = reach(_level)
    TRACE_AT.append(TRACE_AT[-1] + (_high - _low) * SUB)


def trace_place(level):
    start = TRACE_AT[level % SIDE]
    return pl.ds(start, TRACE_AT[level % SIDE + 1] - start)


KEPT = [(level, plane) for level in range(6) for plane in sorted({level, level + 1, 10 - level, 11 - level})]
EARLY_KEPT = {pair: i for i, pair in enumerate(pair for pair in KEPT if pair[0] < SIDE)}
LATE_KEPT = {pair: i for i, pair in enumerate(pair for pair in KEPT if pair[0] >= SIDE)}


def span_sum(cells):
    lane = lax.broadcasted_iota(jnp.int32, (1, SUB, LANES), 2)
    row = lax.broadcasted_iota(jnp.int32, (1, SUB, LANES), 1)
    first = lane == 0
    last = lane == LANES - 1
    corner = (first & (row == 0)) | (last & (row == SUB - 1))
    after = pltpu.roll(cells, LANES - 1, 2)
    before = pltpu.roll(cells, 1, 2)
    carry = jnp.where(last, pltpu.roll(after, SUB - 1, 1), pltpu.roll(before, 1, 1))
    carry = jnp.where(corner, 0.0, carry)
    return jnp.where(last, carry, after) + jnp.where(first, carry, before)


def split_cells(values):
    high = values.astype(jnp.bfloat16)
    low = (values - high.astype(jnp.float32)).astype(jnp.bfloat16)
    return high, low


def weights(couple_ref):
    high, low = split_cells(couple_ref[...])
    return jnp.concatenate([high, high, low], axis=0)


def advance(src, dst, conduct, code, weight, first, count, low, high):
    rows = high - low
    at = pl.ds(low * SUB, rows * SUB)
    mid = pl.ds(first + 1, count)
    here = src[mid, at, :]
    around = (
        src[pl.ds(first, count), at, :]
        + src[pl.ds(first + 2, count), at, :]
        + src[mid, pl.ds((low - 1) * SUB, rows * SUB), :]
        + src[mid, pl.ds((low + 1) * SUB, rows * SUB), :]
    )
    along = span_sum(here.reshape(count * rows, SUB, LANES)).reshape(here.shape)
    flat = here.reshape(count * rows * SUB, LANES)
    near, rest = split_cells(flat)
    product = jnp.dot(
        jnp.concatenate([near, rest, near], axis=1), weight, preferred_element_type=jnp.float32
    )
    plane = pl.ds(first, count)
    marks = code[plane, at, :]
    penalty = jnp.where(
        marks == 1.0,
        product[:, :LANES].reshape(here.shape),
        jnp.where(marks == 2.0, product[:, LANES:].reshape(here.shape), 0.0),
    )
    dst[mid, at, :] = here + conduct[plane, at, :] * (around + along - 6.0 * here) - penalty


def advance_groups(src, dst, conduct, code, weight, groups, count, stride, low, high):
    for i in range(groups):
        advance(src, dst, conduct, code, weight, i * stride, count, low, high)


def inside(axis):
    place = lax.axis_index(axis)
    return place > 0, place < lax.axis_size(axis) - 1


def kept_if(flag, values):
    return jnp.where(flag, values, 0.0)


def odd_place(axis):
    return lax.axis_index(axis) % 2 == 1


def send(first, second, at, upward, downward, axis="xy"):
    odd = odd_place(axis)
    first[at] = jnp.where(odd, upward, downward)
    second[at] = jnp.where(odd, downward, upward)


def got(first, second, at, from_before, axis="xy"):
    return jnp.where(odd_place(axis) == from_before, second[at], first[at])


def spread(block, dst, offset, at_plane, planes=range(PLANES)):
    for plane in planes:
        for chunk in range(CHUNKS):
            dst[plane + at_plane, pl.ds(offset * SUB + chunk, OWN, stride=SUB), :] = block[
                plane, :, chunk * LANES : (chunk + 1) * LANES
            ]


def widened(codes):
    tile_of = lax.broadcasted_iota(jnp.int32, (LANES, CHUNKS * LANES), 0)
    cell_of = lax.broadcasted_iota(jnp.int32, (LANES, CHUNKS * LANES), 1)
    widen = jnp.where(tile_of == cell_of // TILE, 1.0, 0.0).astype(jnp.bfloat16)
    flat = codes.reshape(-1, LANES).astype(jnp.bfloat16)
    wide = jnp.dot(flat, widen, preferred_element_type=jnp.float32)
    return wide.reshape(codes.shape[0], OWN, CHUNKS * LANES)


def ghosts(src, low, high, from_below=None, from_above=None):
    at = span(low, high)
    if from_below is None:
        src[0, at, :] = src[1, at, :] * 0.6
        src[PLANES + 1, at, :] = src[PLANES, at, :] * 0.6
    else:
        src[0, at, :] = (from_below + 0.75 * src[1, at, :]) * 0.8
        src[PLANES + 1, at, :] = (from_above + 0.75 * src[PLANES, at, :]) * 0.8


def put_traces(src, first, second, level):
    at = span(*reach(level))
    place = trace_place(level)
    to_below = 0.75 * src[2, at, :] - 0.25 * src[1, at, :]
    to_above = 0.75 * src[PLANES - 1, at, :] - 0.25 * src[PLANES, at, :]
    send(first, second, place, to_above, to_below, "zg")


def prepare_kernel(
    start_field, diffusivity, tile_block, block_material,
    first, second, code,
    own_v, own_d, own_t, material, tiles, field, conduct, arrived,
):
    copies = [
        pltpu.make_async_copy(source, target, arrived.at[i])
        for i, (source, target) in enumerate(
            ((start_field, own_v), (diffusivity, own_d), (tile_block, own_t), (block_material, material))
        )
    ]
    for copy in copies:
        copy.start()
    copies[0].wait()
    spread(own_v, field, 0, 0)
    copies[1].wait()
    spread(own_d, conduct, 0, 0)
    copies[2].wait()
    copies[3].wait()
    tiles[...] = jnp.zeros(tiles.shape, jnp.int32)
    tiles[:, :, : own_t.shape[2]] = own_t[...]
    table = material[...]
    row = lax.broadcasted_iota(jnp.int32, (SUB, LANES), 0)
    bits = jnp.zeros((SUB, LANES), jnp.int32)
    for part in range(table.shape[0] // SUB):
        bits = bits + (table[part * SUB : (part + 1) * SUB] << (row + part * SUB))
    for shift in (4, 2, 1):
        bits = bits + pltpu.roll(bits, shift, 0)
    for plane in range(PLANES):
        block = tiles[plane]
        entry = jnp.maximum(block - 1, 0)
        word = jnp.take_along_axis(bits, entry & (LANES - 1), axis=1)
        kind = (word >> (entry >> 7)) & 1
        code[plane] = jnp.where(block > 0, kind + 1, 0).astype(jnp.float32)
        at = plane * NEAR
        send(first, second, pl.ds(at, HALF), field[plane, HALF:, :], field[plane, :HALF, :])
        send(
            first, second, pl.ds(at + HALF, REST),
            conduct[plane, OWN_ROWS - REST :, :], conduct[plane, :REST, :],
        )
        send(first, second, pl.ds(CODES_AT + 3 * plane, 3), code[plane, 5:, :], code[plane, :3, :])
    for packet in (first, second):
        packet[CODES_AT + 3 * PLANES :, :] = jnp.zeros((4, LANES), jnp.float32)


def own_kernel(start_field, diffusivity, code, even, factor, marks, wide):
    spread(start_field, even, HALO, 0)
    spread(diffusivity, factor, HALO, 0)
    wide[...] = widened(code[...])
    spread(wide, marks, HALO, 0)


def keep(src, kept, places, level):
    low, high = reach(level)
    at = span(low - 1, high + 1)
    for plane in range(PLANES):
        if (level, plane) in places:
            kept[places[level, plane], at, :] = src[plane + 1, at, :]


def first_kernel(
    near_first, near_second, field, conduct, code, couple,
    first, second, trace_first, trace_second, state, kept, factor, marks,
    even, odd, wide, codes,
):
    weight = weights(couple)
    has_left, has_right = inside("xy")
    own = pl.ds(OWN_AT, OWN_ROWS)
    for flag, from_left, offset, near_at, rest_at, place in (
        (has_left, True, 0, 4 * SUB, 5 * SUB, 5),
        (has_right, False, HALO + OWN, 16 * SUB, 16 * SUB, 0),
    ):
        def packet(at, size):
            return kept_if(flag, got(near_first, near_second, pl.ds(at, size), from_left))

        codes[...] = jnp.zeros(codes.shape, jnp.float32)
        for plane in range(PLANES):
            at = plane * NEAR
            even[plane + 1, pl.ds(near_at, HALF), :] = packet(at, HALF)
            factor[plane, pl.ds(rest_at, REST), :] = packet(at + HALF, REST)
            codes[plane, place : place + 3, :] = packet(CODES_AT + 3 * plane, 3)
        wide[...] = widened(codes[...])
        spread(wide, marks, offset, 0)
    even[1 : PLANES + 1, own, :] = field[:, own, :]
    factor[:, own, :] = conduct[:, own, :]
    marks[:, own, :] = code[:, own, :]
    buffers = (even, odd)
    for level in range(SIDE):
        src, dst = buffers[level % 2], buffers[1 - level % 2]
        put_traces(src, trace_first, trace_second, level)
        keep(src, kept, EARLY_KEPT, level)
        low, high = reach(level)
        ghosts(src, low, high)
        advance_groups(src, dst, factor, marks, weight, 1, PLANES, 0, low, high)
    state[...] = even[1 : PLANES + 1, OWN_AT : OWN_AT + OWN_ROWS, :]
    for i, plane in enumerate(EDGE_PLANES):
        at = i * REST
        send(first, second, pl.ds(at, REST), state[plane, OWN_ROWS - REST :, :], state[plane, :REST, :])
    for i, plane in enumerate(INNER_PLANES):
        at = INNER_AT + i * HALF
        send(first, second, pl.ds(at, HALF), state[plane, HALF:, :], state[plane, :HALF, :])


def middle_kernel(
    first, second, state, factor, marks, couple,
    trace_first, trace_second, kept,
    even, odd,
):
    weight = weights(couple)
    has_left, has_right = inside("xy")
    for plane in range(PLANES):
        even[plane + 1, pl.ds(OWN_AT, OWN_ROWS), :] = state[plane]
    for i, plane in enumerate(EDGE_PLANES):
        at = i * REST
        at = pl.ds(at, REST)
        even[plane + 1, pl.ds(5 * SUB, REST), :] = kept_if(has_left, got(first, second, at, True))
        even[plane + 1, pl.ds(16 * SUB, REST), :] = kept_if(has_right, got(first, second, at, False))
    for i, plane in enumerate(INNER_PLANES):
        at = INNER_AT + i * HALF
        at = pl.ds(at, HALF)
        even[plane + 1, pl.ds(4 * SUB, HALF), :] = kept_if(has_left, got(first, second, at, True))
        even[plane + 1, pl.ds(16 * SUB, HALF), :] = kept_if(has_right, got(first, second, at, False))
    buffers = (even, odd)
    for level in range(SIDE, STEPS):
        src, dst = buffers[level % 2], buffers[1 - level % 2]
        put_traces(src, trace_first, trace_second, level)
        keep(src, kept, LATE_KEPT, level)
        if level == STEPS - 1:
            break
        low, high = reach(level)
        ghosts(src, low + 1, high - 1)
        count = STEPS - level
        advance_groups(src, dst, factor, marks, weight, 2, count, PLANES - count, low + 1, high - 1)
        if level == SIDE:
            advance(src, dst, factor, marks, weight, 5, 2, low, high)


def second_steps(levels, buffers, kept, places, trace_first, trace_second, factor, marks, weight):
    has_below, has_above = inside("zg")
    for level in levels:
        src, dst = buffers[level % 2], buffers[1 - level % 2]
        low, high = reach(level)
        for plane in range(PLANES):
            if (level, plane) in places:
                at = span(low - 1, high + 1)
                src[plane + 1, at, :] = kept[places[level, plane], at, :]
        place = trace_place(level)
        ghosts(
            src, low, high,
            kept_if(has_below, got(trace_first, trace_second, place, True, "zg")),
            kept_if(has_above, got(trace_first, trace_second, place, False, "zg")),
        )
        groups, count, stride = (2, level + 1, 11 - level) if level < 5 else (1, PLANES, 0)
        advance_groups(src, dst, factor, marks, weight, groups, count, stride, low, high)


def second_kernel(
    trace_first, trace_second, kept, factor, marks, couple,
    first, second, state,
    even, odd,
):
    second_steps(range(SIDE), (even, odd), kept, EARLY_KEPT, trace_first, trace_second, factor, marks, weights(couple))
    for i, plane in enumerate(EDGE_PLANES):
        state[i] = even[plane + 1, pl.ds(OWN_AT, OWN_ROWS), :]
        send(first, second, i, state[i, HALF:, :], state[i, :HALF, :])


def last_kernel(
    trace_first, trace_second, first, second, state, kept, factor, marks, couple,
    result,
    even, odd,
):
    has_left, has_right = inside("xy")
    for i, plane in enumerate(EDGE_PLANES):
        even[plane + 1, pl.ds(OWN_AT, OWN_ROWS), :] = state[i]
        even[plane + 1, pl.ds(OWN_AT - HALF, HALF), :] = kept_if(has_left, got(first, second, i, True))
        even[plane + 1, pl.ds(OWN_AT + OWN_ROWS, HALF), :] = kept_if(has_right, got(first, second, i, False))
    second_steps(
        range(SIDE, STEPS), (even, odd), kept, LATE_KEPT, trace_first, trace_second, factor, marks,
        weights(couple),
    )
    for plane in range(PLANES):
        for chunk in range(CHUNKS):
            result[plane, :, chunk * LANES : (chunk + 1) * LANES] = even[
                plane + 1, pl.ds(OWN_AT + chunk, OWN, stride=SUB), :
            ]


def shape(*dims):
    return jax.ShapeDtypeStruct(dims, jnp.float32)


VMEM = pl.BlockSpec(memory_space=pltpu.VMEM)
FIELD = (PLANES, ROWS * SUB, LANES)
PADDED = (PLANES + 2, ROWS * SUB, LANES)
CELLS = (PLANES, OWN_ROWS, LANES)
TRACES = (TRACE_AT[-1], LANES)
WIDE = (PLANES, OWN, CHUNKS * LANES)
PACKET = (CODES_AT + 3 * PLANES + 4, LANES)
SHARE = (INNER_AT + len(INNER_PLANES) * HALF, LANES)
EDGE_SHARE = (len(EDGE_PLANES), HALF, LANES)


def call(kernel, outs, scratch, *operands, place=VMEM, limit=VMEM_LIMIT):
    return pl.pallas_call(
        kernel,
        out_shape=[shape(*dims) for dims in outs],
        in_specs=[place] * len(operands),
        out_specs=[VMEM] * len(outs),
        scratch_shapes=scratch,
        compiler_params=pltpu.CompilerParams(vmem_limit_bytes=limit),
        name=kernel.__name__,
    )(*operands)


def scratch(*shapes):
    return [pltpu.VMEM(dims, jnp.float32) for dims in shapes]


def swap(first, second, axis):
    levels, lines = lax.axis_size("zg"), lax.axis_size("xy")
    count = lax.axis_size(axis)

    def device(along, other):
        return along * lines + other if axis == "zg" else other * lines + along

    shifted, pairs = [], []
    for other in range(levels * lines // count):
        shifted += [(device(i, other), device(i + 1, other)) for i in range(1, count - 1, 2)]
        pairs += [(device(i, other), device(i + 1, other)) for i in range(0, count, 2)]
        idle = other ^ 1 if axis == "zg" else other ^ 4
        if idle > other:
            shifted += [(device(i, other), device(i, idle)) for i in (0, count - 1)]
    return tuple(
        lax.ppermute(cells, ("zg", "xy"), pairing + [(j, i) for i, j in pairing])
        for cells, pairing in ((first, shifted), (second, pairs))
    )


def on_device(start_field, diffusivity, tile_block, block_material, material_coupling):
    turned = jnp.swapaxes(material_coupling, 1, 2)
    empty = jnp.zeros((TILE, TILE), jnp.float32)
    couple = jnp.concatenate(
        [jnp.block([[turned[kind], empty], [empty, turned[kind]]]) for kind in (0, 1)], axis=1
    )
    material = block_material.reshape(-1, LANES)
    first, second, code = call(
        prepare_kernel,
        [PACKET, PACKET, (PLANES, OWN, LANES)],
        scratch(start_field.shape, diffusivity.shape)
        + [
            pltpu.VMEM(tile_block.shape, jnp.int32),
            pltpu.VMEM(material.shape, jnp.int32),
            pltpu.VMEM((PLANES, OWN, LANES), jnp.int32),
        ]
        + scratch(CELLS, CELLS)
        + [pltpu.SemaphoreType.DMA((4,))],
        start_field, diffusivity, tile_block, material,
        place=pl.BlockSpec(memory_space=pltpu.HBM),
        limit=56 * 1024 * 1024,
    )
    near = swap(first, second, "xy")
    field, conduct, code = call(
        own_kernel, [FIELD] * 3, scratch(WIDE), start_field, diffusivity, code
    )
    first, second, trace_first, trace_second, state, early_kept, factor, marks = call(
        first_kernel,
        [SHARE, SHARE, TRACES, TRACES, CELLS, (len(EARLY_KEPT), ROWS * SUB, LANES), FIELD, FIELD],
        scratch(PADDED, PADDED, WIDE, (PLANES, OWN, LANES)),
        *near, field, conduct, code, couple,
    )
    sides = swap(first, second, "xy")
    early = swap(trace_first, trace_second, "zg")
    trace_first, trace_second, late_kept = call(
        middle_kernel,
        [TRACES, TRACES, (len(LATE_KEPT), ROWS * SUB, LANES)],
        scratch(PADDED, PADDED),
        *sides, state, factor, marks, couple,
    )
    late = swap(trace_first, trace_second, "zg")
    first, second, state = call(
        second_kernel,
        [EDGE_SHARE, EDGE_SHARE, (len(EDGE_PLANES), OWN_ROWS, LANES)],
        scratch(PADDED, PADDED),
        *early, early_kept, factor, marks, couple,
    )
    sides = swap(first, second, "xy")
    (result,) = call(
        last_kernel,
        [start_field.shape],
        scratch(PADDED, PADDED),
        *late, *sides, state, late_kept, factor, marks, couple,
    )
    return result


def solution(mesh):
    return jax.shard_map(
        on_device,
        mesh=mesh,
        in_specs=(P("zg", "xy", None), P("zg", "xy", None), P("zg", "xy", None), P(), P()),
        out_specs=P("zg", "xy", None),
        check_vma=False,
    )
```

```python
import jax
import jax.numpy as jnp
from jax import lax
from jax.experimental import pallas as pl
from jax.experimental.pallas import tpu as pltpu
from jax.sharding import PartitionSpec as P

TILE = 64
STEPS = 8
PLANES = 12
OWN = 8
HALO = 8
ROWS = OWN + 2 * HALO
SUB = 8
LANES = 128
CHUNKS = 8
VMEM_LIMIT = 24 * 1024 * 1024


SIDE = 4
OWN_AT = HALO * SUB
OWN_ROWS = OWN * SUB
HALF = SIDE * SUB
EDGE_PLANES = (0, 1, 2, 3, 8, 9, 10, 11)
REST = 3 * SUB
NEAR = HALF + REST
CODES_AT = PLANES * NEAR
RENEWED = (3, 3, 2, 1, 4, 4, 4, 4, 1, 2, 3, 3)
RENEWED_AT = [SUB * sum(RENEWED[:plane]) for plane in range(PLANES + 1)]


def reach(level):
    margin = HALO - SIDE + 1 + level % SIDE
    return margin, ROWS - margin


def span(low, high):
    return pl.ds(low * SUB, (high - low) * SUB)


TRACE_AT = [0]
for _level in range(SIDE):
    _low, _high = reach(_level)
    TRACE_AT.append(TRACE_AT[-1] + (_high - _low) * SUB)


def trace_place(level):
    start = TRACE_AT[level % SIDE]
    return pl.ds(start, TRACE_AT[level % SIDE + 1] - start)


KEPT = [(level, plane) for level in range(6) for plane in sorted({level, level + 1, 10 - level, 11 - level})]
EARLY_KEPT = {pair: i for i, pair in enumerate(pair for pair in KEPT if pair[0] < SIDE)}
LATE_KEPT = {pair: i for i, pair in enumerate(pair for pair in KEPT if pair[0] >= SIDE)}


def span_sum(cells):
    lane = lax.broadcasted_iota(jnp.int32, (1, SUB, LANES), 2)
    row = lax.broadcasted_iota(jnp.int32, (1, SUB, LANES), 1)
    after = jnp.where(row == SUB - 1, 0.0, pltpu.roll(cells, SUB - 1, 1))
    before = jnp.where(row == 0, 0.0, pltpu.roll(cells, 1, 1))
    return pltpu.roll(jnp.where(lane == 0, after, cells), LANES - 1, 2) + pltpu.roll(
        jnp.where(lane == LANES - 1, before, cells), 1, 2
    )


def split_cells(values):
    high = values.astype(jnp.bfloat16)
    low = (values - high.astype(jnp.float32)).astype(jnp.bfloat16)
    return high, low


def weights(couple_ref):
    high, low = split_cells(couple_ref[...])
    return jnp.concatenate([high, high, low], axis=0)


def advance(src, dst, conduct, code, weight, first, count, low, high):
    rows = high - low
    at = pl.ds(low * SUB, rows * SUB)
    mid = pl.ds(first + 1, count)
    here = src[mid, at, :]
    around = (
        src[pl.ds(first, count), at, :]
        + src[pl.ds(first + 2, count), at, :]
        + src[mid, pl.ds((low - 1) * SUB, rows * SUB), :]
        + src[mid, pl.ds((low + 1) * SUB, rows * SUB), :]
    )
    along = span_sum(here.reshape(count * rows, SUB, LANES)).reshape(here.shape)
    flat = here.reshape(count * rows * SUB, LANES)
    near, rest = split_cells(flat)
    product = jnp.dot(
        jnp.concatenate([near, rest, near], axis=1), weight, preferred_element_type=jnp.float32
    )
    plane = pl.ds(first, count)
    marks = code[plane, at, :]
    penalty = jnp.where(
        marks == 1.0,
        product[:, :LANES].reshape(here.shape),
        jnp.where(marks == 2.0, product[:, LANES:].reshape(here.shape), 0.0),
    )
    dst[mid, at, :] = here + conduct[plane, at, :] * (around + along - 6.0 * here) - penalty


def advance_groups(src, dst, conduct, code, weight, groups, count, stride, low, high):
    for i in range(groups):
        advance(src, dst, conduct, code, weight, i * stride, count, low, high)


def inside(axis):
    place = lax.axis_index(axis)
    return place > 0, place < lax.axis_size(axis) - 1


def kept_if(flag, values):
    return jnp.where(flag, values, 0.0)


def odd_place(axis):
    return lax.axis_index(axis) % 2 == 1


def send(first, second, at, upward, downward, axis="xy"):
    odd = odd_place(axis)
    first[at] = jnp.where(odd, upward, downward)
    second[at] = jnp.where(odd, downward, upward)


def got(first, second, at, from_before, axis="xy"):
    return jnp.where(odd_place(axis) == from_before, second[at], first[at])


def spread(block, dst, offset, at_plane, planes=range(PLANES)):
    for plane in planes:
        for chunk in range(CHUNKS):
            dst[plane + at_plane, pl.ds(offset * SUB + chunk, OWN, stride=SUB), :] = block[
                plane, :, chunk * LANES : (chunk + 1) * LANES
            ]


def widened(codes):
    tile_of = lax.broadcasted_iota(jnp.int32, (LANES, CHUNKS * LANES), 0)
    cell_of = lax.broadcasted_iota(jnp.int32, (LANES, CHUNKS * LANES), 1)
    widen = jnp.where(tile_of == cell_of // TILE, 1.0, 0.0).astype(jnp.bfloat16)
    flat = codes.reshape(-1, LANES).astype(jnp.bfloat16)
    wide = jnp.dot(flat, widen, preferred_element_type=jnp.float32)
    return wide.reshape(codes.shape[0], OWN, CHUNKS * LANES)


def ghosts(src, low, high, from_below=None, from_above=None):
    at = span(low, high)
    if from_below is None:
        src[0, at, :] = src[1, at, :] * 0.6
        src[PLANES + 1, at, :] = src[PLANES, at, :] * 0.6
    else:
        src[0, at, :] = (from_below + 0.75 * src[1, at, :]) * 0.8
        src[PLANES + 1, at, :] = (from_above + 0.75 * src[PLANES, at, :]) * 0.8


def put_traces(src, first, second, level):
    at = span(*reach(level))
    place = trace_place(level)
    to_below = 0.75 * src[2, at, :] - 0.25 * src[1, at, :]
    to_above = 0.75 * src[PLANES - 1, at, :] - 0.25 * src[PLANES, at, :]
    send(first, second, place, to_above, to_below, "zg")


def prepare_kernel(
    start_field, diffusivity, tile_block, block_material,
    first, second, code,
    own_v, own_d, own_t, material, tiles, field, conduct, to_first, to_second, codes, arrived, left,
):
    half = PLANES // 2
    loads = [
        pltpu.make_async_copy(tile_block, own_t, arrived.at[0]),
        pltpu.make_async_copy(block_material, material, arrived.at[1]),
    ]
    for i, (source, target) in enumerate(((start_field, own_v), (diffusivity, own_d))):
        for part in range(2):
            at = pl.ds(part * half, half)
            loads.append(
                pltpu.make_async_copy(source.at[at], target.at[at], arrived.at[2 + 2 * i + part])
            )
    for load in loads:
        load.start()
    stores = []

    def leave(source, target):
        store = pltpu.make_async_copy(source, target, left.at[len(stores)])
        store.start()
        stores.append(store)

    loads[0].wait()
    loads[1].wait()
    tiles[...] = jnp.zeros(tiles.shape, jnp.int32)
    tiles[:, :, : own_t.shape[2]] = own_t[...]
    table = material[...]
    row = lax.broadcasted_iota(jnp.int32, (SUB, LANES), 0)
    bits = jnp.zeros((SUB, LANES), jnp.int32)
    for part in range(table.shape[0] // SUB):
        bits = bits + (table[part * SUB : (part + 1) * SUB] << (row + part * SUB))
    for shift in (4, 2, 1):
        bits = bits + pltpu.roll(bits, shift, 0)
    for plane in range(PLANES):
        block = tiles[plane]
        entry = jnp.maximum(block - 1, 0)
        word = jnp.take_along_axis(bits, entry & (LANES - 1), axis=1)
        kind = (word >> (entry >> 7)) & 1
        codes[plane] = jnp.where(block > 0, kind + 1, 0).astype(jnp.float32)
        send(
            to_first, to_second, pl.ds(CODES_AT + 3 * plane, 3),
            codes[plane, 5:, :], codes[plane, :3, :],
        )
    for packet in (to_first, to_second):
        packet[CODES_AT + 3 * PLANES :, :] = jnp.zeros((4, LANES), jnp.float32)
    leave(codes, code)
    for part in range(2):
        planes = range(part * half, part * half + half)
        loads[2 + part].wait()
        spread(own_v, field, 0, 0, planes)
        loads[4 + part].wait()
        spread(own_d, conduct, 0, 0, planes)
        for plane in planes:
            at = plane * NEAR
            send(to_first, to_second, pl.ds(at, HALF), field[plane, HALF:, :], field[plane, :HALF, :])
            send(
                to_first, to_second, pl.ds(at + HALF, REST),
                conduct[plane, OWN_ROWS - REST :, :], conduct[plane, :REST, :],
            )
        at = pl.ds(0, half * NEAR) if part == 0 else pl.ds(half * NEAR, first.shape[0] - half * NEAR)
        leave(to_first.at[at], first.at[at])
        leave(to_second.at[at], second.at[at])
    for store in stores:
        store.wait()


def own_kernel(start_field, diffusivity, code, even, factor, marks, wide):
    spread(start_field, even, HALO, 0)
    spread(diffusivity, factor, HALO, 0)
    wide[...] = widened(code[...])
    spread(wide, marks, HALO, 0)


def keep(src, kept, places, level):
    low, high = reach(level)
    at = span(low - 1, high + 1)
    for plane in range(PLANES):
        if (level, plane) in places:
            kept[places[level, plane], at, :] = src[plane + 1, at, :]


def first_kernel(
    near_first, near_second, field, conduct, code, couple,
    first, second, trace_first, trace_second, state, kept, factor, marks,
    even, odd, wide, codes,
):
    weight = weights(couple)
    has_left, has_right = inside("xy")
    own = pl.ds(OWN_AT, OWN_ROWS)
    for flag, from_left, offset, near_at, rest_at, place in (
        (has_left, True, 0, 4 * SUB, 5 * SUB, 5),
        (has_right, False, HALO + OWN, 16 * SUB, 16 * SUB, 0),
    ):
        def packet(at, size):
            return kept_if(flag, got(near_first, near_second, pl.ds(at, size), from_left))

        codes[...] = jnp.zeros(codes.shape, jnp.float32)
        for plane in range(PLANES):
            at = plane * NEAR
            even[plane + 1, pl.ds(near_at, HALF), :] = packet(at, HALF)
            factor[plane, pl.ds(rest_at, REST), :] = packet(at + HALF, REST)
            codes[plane, place : place + 3, :] = packet(CODES_AT + 3 * plane, 3)
        wide[...] = widened(codes[...])
        spread(wide, marks, offset, 0)
    even[1 : PLANES + 1, own, :] = field[:, own, :]
    factor[:, own, :] = conduct[:, own, :]
    marks[:, own, :] = code[:, own, :]
    buffers = (even, odd)
    for level in range(SIDE):
        src, dst = buffers[level % 2], buffers[1 - level % 2]
        put_traces(src, trace_first, trace_second, level)
        keep(src, kept, EARLY_KEPT, level)
        low, high = reach(level)
        ghosts(src, low, high)
        advance_groups(src, dst, factor, marks, weight, 3, 4, 4, low, high)
    state[...] = even[1 : PLANES + 1, OWN_AT : OWN_AT + OWN_ROWS, :]
    for plane in range(PLANES):
        rows = RENEWED[plane] * SUB
        send(
            first, second, pl.ds(RENEWED_AT[plane], rows),
            state[plane, OWN_ROWS - rows :, :], state[plane, :rows, :],
        )


def middle_kernel(
    first, second, state, factor, marks, couple,
    trace_first, trace_second, kept,
    even, odd,
):
    weight = weights(couple)
    has_left, has_right = inside("xy")
    for plane in range(PLANES):
        rows = RENEWED[plane] * SUB
        at = pl.ds(RENEWED_AT[plane], rows)
        even[plane + 1, pl.ds(5 * SUB, REST), :] = jnp.zeros((REST, LANES), jnp.float32)
        even[plane + 1, pl.ds(16 * SUB, REST), :] = jnp.zeros((REST, LANES), jnp.float32)
        even[plane + 1, pl.ds(OWN_AT, OWN_ROWS), :] = state[plane]
        even[plane + 1, pl.ds(OWN_AT - rows, rows), :] = kept_if(has_left, got(first, second, at, True))
        even[plane + 1, pl.ds(16 * SUB, rows), :] = kept_if(has_right, got(first, second, at, False))
    buffers = (even, odd)
    for level in range(SIDE, STEPS):
        src, dst = buffers[level % 2], buffers[1 - level % 2]
        put_traces(src, trace_first, trace_second, level)
        keep(src, kept, LATE_KEPT, level)
        if level == STEPS - 1:
            break
        low, high = reach(level)
        ghosts(src, low + 1, high - 1)
        count = STEPS - level
        advance_groups(src, dst, factor, marks, weight, 2, count, PLANES - count, low + 1, high - 1)
        if level == SIDE:
            advance(src, dst, factor, marks, weight, 5, 2, low, high)


def second_steps(levels, buffers, kept, places, trace_first, trace_second, factor, marks, weight):
    has_below, has_above = inside("zg")
    for level in levels:
        src, dst = buffers[level % 2], buffers[1 - level % 2]
        low, high = reach(level)
        for plane in range(PLANES):
            if (level, plane) in places:
                at = span(low - 1, high + 1)
                src[plane + 1, at, :] = kept[places[level, plane], at, :]
        place = trace_place(level)
        ghosts(
            src, low, high,
            kept_if(has_below, got(trace_first, trace_second, place, True, "zg")),
            kept_if(has_above, got(trace_first, trace_second, place, False, "zg")),
        )
        groups, count, stride = (2, level + 1, 11 - level) if level < 5 else (3, 4, 4)
        advance_groups(src, dst, factor, marks, weight, groups, count, stride, low, high)


def second_kernel(
    trace_first, trace_second, kept, factor, marks, couple,
    first, second, state,
    even, odd,
):
    second_steps(range(SIDE), (even, odd), kept, EARLY_KEPT, trace_first, trace_second, factor, marks, weights(couple))
    for i, plane in enumerate(EDGE_PLANES):
        state[i] = even[plane + 1, pl.ds(OWN_AT, OWN_ROWS), :]
        send(first, second, i, state[i, HALF:, :], state[i, :HALF, :])


def last_kernel(
    trace_first, trace_second, first, second, state, kept, factor, marks, couple,
    result,
    even, odd,
):
    has_left, has_right = inside("xy")
    for i, plane in enumerate(EDGE_PLANES):
        even[plane + 1, pl.ds(OWN_AT, OWN_ROWS), :] = state[i]
        even[plane + 1, pl.ds(OWN_AT - HALF, HALF), :] = kept_if(has_left, got(first, second, i, True))
        even[plane + 1, pl.ds(OWN_AT + OWN_ROWS, HALF), :] = kept_if(has_right, got(first, second, i, False))
    second_steps(
        range(SIDE, STEPS), (even, odd), kept, LATE_KEPT, trace_first, trace_second, factor, marks,
        weights(couple),
    )
    for plane in range(PLANES):
        for chunk in range(CHUNKS):
            result[plane, :, chunk * LANES : (chunk + 1) * LANES] = even[
                plane + 1, pl.ds(OWN_AT + chunk, OWN, stride=SUB), :
            ]


def shape(*dims):
    return jax.ShapeDtypeStruct(dims, jnp.float32)


VMEM = pl.BlockSpec(memory_space=pltpu.VMEM)
HBM = pl.BlockSpec(memory_space=pltpu.HBM)
FIELD = (PLANES, ROWS * SUB, LANES)
PADDED = (PLANES + 2, ROWS * SUB, LANES)
CELLS = (PLANES, OWN_ROWS, LANES)
TRACES = (TRACE_AT[-1], LANES)
WIDE = (PLANES, OWN, CHUNKS * LANES)
PACKET = (CODES_AT + 3 * PLANES + 4, LANES)
SHARE = (RENEWED_AT[-1], LANES)
EDGE_SHARE = (len(EDGE_PLANES), HALF, LANES)


def call(kernel, outs, scratch, *operands, place=VMEM, out_place=VMEM, limit=VMEM_LIMIT):
    return pl.pallas_call(
        kernel,
        out_shape=[shape(*dims) for dims in outs],
        in_specs=[place] * len(operands),
        out_specs=[out_place] * len(outs),
        scratch_shapes=scratch,
        compiler_params=pltpu.CompilerParams(vmem_limit_bytes=limit),
        name=kernel.__name__,
    )(*operands)


def scratch(*shapes):
    return [pltpu.VMEM(dims, jnp.float32) for dims in shapes]


def swap(first, second, axis):
    levels, lines = lax.axis_size("zg"), lax.axis_size("xy")
    count = lax.axis_size(axis)

    def device(along, other):
        return along * lines + other if axis == "zg" else other * lines + along

    shifted, pairs = [], []
    for other in range(levels * lines // count):
        shifted += [(device(i, other), device(i + 1, other)) for i in range(1, count - 1, 2)]
        pairs += [(device(i, other), device(i + 1, other)) for i in range(0, count, 2)]
        idle = other ^ 1 if axis == "zg" else other ^ 4
        if idle > other:
            shifted += [(device(i, other), device(i, idle)) for i in (0, count - 1)]
    return tuple(
        lax.ppermute(cells, ("zg", "xy"), pairing + [(j, i) for i, j in pairing])
        for cells, pairing in ((first, shifted), (second, pairs))
    )


def on_device(start_field, diffusivity, tile_block, block_material, material_coupling):
    turned = jnp.swapaxes(material_coupling, 1, 2)
    empty = jnp.zeros((TILE, TILE), jnp.float32)
    couple = jnp.concatenate(
        [jnp.block([[turned[kind], empty], [empty, turned[kind]]]) for kind in (0, 1)], axis=1
    )
    material = block_material.reshape(-1, LANES)
    first, second, code = call(
        prepare_kernel,
        [PACKET, PACKET, (PLANES, OWN, LANES)],
        scratch(start_field.shape, diffusivity.shape)
        + [
            pltpu.VMEM(tile_block.shape, jnp.int32),
            pltpu.VMEM(material.shape, jnp.int32),
            pltpu.VMEM((PLANES, OWN, LANES), jnp.int32),
        ]
        + scratch(CELLS, CELLS, PACKET, PACKET, (PLANES, OWN, LANES))
        + [pltpu.SemaphoreType.DMA((6,)), pltpu.SemaphoreType.DMA((5,))],
        start_field, diffusivity, tile_block, material,
        place=HBM,
        out_place=HBM,
        limit=56 * 1024 * 1024,
    )
    near = swap(first, second, "xy")
    field, conduct, code = call(
        own_kernel, [FIELD] * 3, scratch(WIDE), start_field, diffusivity, code
    )
    first, second, trace_first, trace_second, state, early_kept, factor, marks = call(
        first_kernel,
        [SHARE, SHARE, TRACES, TRACES, CELLS, (len(EARLY_KEPT), ROWS * SUB, LANES), FIELD, FIELD],
        scratch(PADDED, PADDED, WIDE, (PLANES, OWN, LANES)),
        *near, field, conduct, code, couple,
    )
    sides = swap(first, second, "xy")
    early = swap(trace_first, trace_second, "zg")
    trace_first, trace_second, late_kept = call(
        middle_kernel,
        [TRACES, TRACES, (len(LATE_KEPT), ROWS * SUB, LANES)],
        scratch(PADDED, PADDED),
        *sides, state, factor, marks, couple,
    )
    late = swap(trace_first, trace_second, "zg")
    first, second, state = call(
        second_kernel,
        [EDGE_SHARE, EDGE_SHARE, (len(EDGE_PLANES), OWN_ROWS, LANES)],
        scratch(PADDED, PADDED),
        *early, early_kept, factor, marks, couple,
    )
    sides = swap(first, second, "xy")
    (result,) = call(
        last_kernel,
        [start_field.shape],
        scratch(PADDED, PADDED),
        *late, *sides, state, late_kept, factor, marks, couple,
    )
    return result


def solution(mesh):
    return jax.shard_map(
        on_device,
        mesh=mesh,
        in_specs=(P("zg", "xy", None), P("zg", "xy", None), P("zg", "xy", None), P(), P()),
        out_specs=P("zg", "xy", None),
        check_vma=False,
    )
```

```python
import jax
import jax.numpy as jnp
from jax import lax
from jax.experimental import pallas as pl
from jax.experimental.pallas import tpu as pltpu
from jax.sharding import PartitionSpec as P

TILE = 64
STEPS = 8
PLANES = 12
OWN = 8
HALO = 8
ROWS = OWN + 2 * HALO
SUB = 8
LANES = 128
CHUNKS = 8
VMEM_LIMIT = 24 * 1024 * 1024
PREPARE_LIMIT = 53 * 1024 * 1024


SIDE = 4
OWN_AT = HALO * SUB
OWN_ROWS = OWN * SUB
HALF = SIDE * SUB
EDGE_PLANES = (0, 1, 2, 3, 8, 9, 10, 11)
REST = 3 * SUB
NEAR = HALF + REST
RENEWED = (3, 3, 2, 1, 4, 4, 4, 4, 1, 2, 3, 3)
RENEWED_AT = [SUB * sum(RENEWED[:plane]) for plane in range(PLANES + 1)]


def reach(level):
    margin = HALO - SIDE + 1 + level % SIDE
    return margin, ROWS - margin


def span(low, high):
    return pl.ds(low * SUB, (high - low) * SUB)


TRACE_AT = [0]
for _level in range(SIDE):
    _low, _high = reach(_level)
    TRACE_AT.append(TRACE_AT[-1] + (_high - _low) * SUB)


def trace_place(level):
    start = TRACE_AT[level % SIDE]
    return pl.ds(start, TRACE_AT[level % SIDE + 1] - start)


KEPT = [(level, plane) for level in range(6) for plane in sorted({level, level + 1, 10 - level, 11 - level})]
EARLY_KEPT = {pair: i for i, pair in enumerate(pair for pair in KEPT if pair[0] < SIDE)}
LATE_KEPT = {pair: i for i, pair in enumerate(pair for pair in KEPT if pair[0] >= SIDE)}


def span_sum(cells):
    lane = lax.broadcasted_iota(jnp.int32, (1, SUB, LANES), 2)
    row = lax.broadcasted_iota(jnp.int32, (1, SUB, LANES), 1)
    after = jnp.where(row == SUB - 1, 0.0, pltpu.roll(cells, SUB - 1, 1))
    before = jnp.where(row == 0, 0.0, pltpu.roll(cells, 1, 1))
    return pltpu.roll(jnp.where(lane == 0, after, cells), LANES - 1, 2) + pltpu.roll(
        jnp.where(lane == LANES - 1, before, cells), 1, 2
    )


def split_cells(values):
    high = values.astype(jnp.bfloat16)
    low = (values - high.astype(jnp.float32)).astype(jnp.bfloat16)
    return high, low


def weights(couple_ref):
    high, low = split_cells(couple_ref[...])
    return jnp.concatenate([high, high, low], axis=0)


def advance(src, dst, conduct, code, weight, first, count, low, high):
    rows = high - low
    at = pl.ds(low * SUB, rows * SUB)
    mid = pl.ds(first + 1, count)
    here = src[mid, at, :]
    around = (
        src[pl.ds(first, count), at, :]
        + src[pl.ds(first + 2, count), at, :]
        + src[mid, pl.ds((low - 1) * SUB, rows * SUB), :]
        + src[mid, pl.ds((low + 1) * SUB, rows * SUB), :]
    )
    along = span_sum(here.reshape(count * rows, SUB, LANES)).reshape(here.shape)
    flat = here.reshape(count * rows * SUB, LANES)
    near, rest = split_cells(flat)
    product = jnp.dot(
        jnp.concatenate([near, rest, near], axis=1), weight, preferred_element_type=jnp.float32
    )
    plane = pl.ds(first, count)
    marks = code[plane, at, :]
    penalty = jnp.where(
        marks == 1.0,
        product[:, :LANES].reshape(here.shape),
        jnp.where(marks == 2.0, product[:, LANES:].reshape(here.shape), 0.0),
    )
    dst[mid, at, :] = here + conduct[plane, at, :] * (around + along - 6.0 * here) - penalty


def advance_groups(src, dst, conduct, code, weight, groups, count, stride, low, high):
    for i in range(groups):
        advance(src, dst, conduct, code, weight, i * stride, count, low, high)


def inside(axis):
    place = lax.axis_index(axis)
    return place > 0, place < lax.axis_size(axis) - 1


def kept_if(flag, values):
    return jnp.where(flag, values, 0.0)


def odd_place(axis):
    return lax.axis_index(axis) % 2 == 1


def send(first, second, at, upward, downward, axis="xy"):
    odd = odd_place(axis)
    first[at] = jnp.where(odd, upward, downward)
    second[at] = jnp.where(odd, downward, upward)


def got(first, second, at, from_before, axis="xy"):
    return jnp.where(odd_place(axis) == from_before, second[at], first[at])


def spread(block, dst, offset, at_plane, planes=range(PLANES)):
    for plane in planes:
        for chunk in range(CHUNKS):
            dst[plane + at_plane, pl.ds(offset * SUB + chunk, OWN, stride=SUB), :] = block[
                plane, :, chunk * LANES : (chunk + 1) * LANES
            ]


def widened(codes):
    tile_of = lax.broadcasted_iota(jnp.int32, (LANES, CHUNKS * LANES), 0)
    cell_of = lax.broadcasted_iota(jnp.int32, (LANES, CHUNKS * LANES), 1)
    widen = jnp.where(tile_of == cell_of // TILE, 1.0, 0.0).astype(jnp.bfloat16)
    flat = codes.reshape(-1, LANES).astype(jnp.bfloat16)
    wide = jnp.dot(flat, widen, preferred_element_type=jnp.float32)
    return wide.reshape(codes.shape[0], OWN, CHUNKS * LANES)


def ghosts(src, low, high, from_below=None, from_above=None):
    at = span(low, high)
    if from_below is None:
        src[0, at, :] = src[1, at, :] * 0.6
        src[PLANES + 1, at, :] = src[PLANES, at, :] * 0.6
    else:
        src[0, at, :] = (from_below + 0.75 * src[1, at, :]) * 0.8
        src[PLANES + 1, at, :] = (from_above + 0.75 * src[PLANES, at, :]) * 0.8


def put_traces(src, first, second, level):
    at = span(*reach(level))
    place = trace_place(level)
    to_below = 0.75 * src[2, at, :] - 0.25 * src[1, at, :]
    to_above = 0.75 * src[PLANES - 1, at, :] - 0.25 * src[PLANES, at, :]
    send(first, second, place, to_above, to_below, "zg")


def prepare_kernel(start_field, diffusivity, first, second, own_v, own_d, field, conduct, arrived):
    half = PLANES // 2
    loads = []
    for part in range(2):
        at = pl.ds(part * half, half)
        for source, target in ((start_field, own_v), (diffusivity, own_d)):
            load = pltpu.make_async_copy(source.at[at], target.at[at], arrived.at[len(loads)])
            load.start()
            loads.append(load)
    for part in range(2):
        planes = range(part * half, part * half + half)
        loads[2 * part].wait()
        spread(own_v, field, 0, 0, planes)
        loads[2 * part + 1].wait()
        spread(own_d, conduct, 0, 0, planes)
        for plane in planes:
            at = plane * NEAR
            send(first, second, pl.ds(at, HALF), field[plane, HALF:, :], field[plane, :HALF, :])
            send(
                first, second, pl.ds(at + HALF, REST),
                conduct[plane, OWN_ROWS - REST :, :], conduct[plane, :REST, :],
            )


def code_kernel(tile_block, material, first, second, code, tiles):
    tiles[...] = jnp.zeros(tiles.shape, jnp.int32)
    tiles[:, :, : tile_block.shape[2]] = tile_block[...]
    table = material[...]
    row = lax.broadcasted_iota(jnp.int32, (SUB, LANES), 0)
    bits = jnp.zeros((SUB, LANES), jnp.int32)
    for part in range(table.shape[0] // SUB):
        bits = bits + (table[part * SUB : (part + 1) * SUB] << (row + part * SUB))
    for shift in (4, 2, 1):
        bits = bits + pltpu.roll(bits, shift, 0)
    for plane in range(PLANES):
        block = tiles[plane]
        entry = jnp.maximum(block - 1, 0)
        word = jnp.take_along_axis(bits, entry & (LANES - 1), axis=1)
        kind = (word >> (entry >> 7)) & 1
        code[plane] = jnp.where(block > 0, kind + 1, 0).astype(jnp.float32)
        send(first, second, pl.ds(3 * plane, 3), code[plane, 5:, :], code[plane, :3, :])
    for packet in (first, second):
        packet[3 * PLANES :, :] = jnp.zeros((4, LANES), jnp.float32)


def own_kernel(start_field, diffusivity, code, even, factor, marks, wide):
    spread(start_field, even, HALO, 0)
    spread(diffusivity, factor, HALO, 0)
    wide[...] = widened(code[...])
    spread(wide, marks, HALO, 0)


def keep(src, kept, places, level):
    low, high = reach(level)
    at = span(low - 1, high + 1)
    for plane in range(PLANES):
        if (level, plane) in places:
            kept[places[level, plane], at, :] = src[plane + 1, at, :]


def first_kernel(
    near_first, near_second, code_first, code_second, field, conduct, code, couple,
    first, second, trace_first, trace_second, state, kept, factor, marks,
    even, odd, wide, codes,
):
    weight = weights(couple)
    has_left, has_right = inside("xy")
    own = pl.ds(OWN_AT, OWN_ROWS)
    for flag, from_left, offset, near_at, rest_at, place in (
        (has_left, True, 0, 4 * SUB, 5 * SUB, 5),
        (has_right, False, HALO + OWN, 16 * SUB, 16 * SUB, 0),
    ):
        def packet(at, size):
            return kept_if(flag, got(near_first, near_second, pl.ds(at, size), from_left))

        codes[...] = jnp.zeros(codes.shape, jnp.float32)
        for plane in range(PLANES):
            at = plane * NEAR
            even[plane + 1, pl.ds(near_at, HALF), :] = packet(at, HALF)
            factor[plane, pl.ds(rest_at, REST), :] = packet(at + HALF, REST)
            codes[plane, place : place + 3, :] = kept_if(
                flag, got(code_first, code_second, pl.ds(3 * plane, 3), from_left)
            )
        wide[...] = widened(codes[...])
        spread(wide, marks, offset, 0)
    even[1 : PLANES + 1, own, :] = field[:, own, :]
    factor[:, own, :] = conduct[:, own, :]
    marks[:, own, :] = code[:, own, :]
    buffers = (even, odd)
    for level in range(SIDE):
        src, dst = buffers[level % 2], buffers[1 - level % 2]
        put_traces(src, trace_first, trace_second, level)
        keep(src, kept, EARLY_KEPT, level)
        low, high = reach(level)
        ghosts(src, low, high)
        advance_groups(src, dst, factor, marks, weight, 3, 4, 4, low, high)
    state[...] = even[1 : PLANES + 1, OWN_AT : OWN_AT + OWN_ROWS, :]
    for plane in range(PLANES):
        rows = RENEWED[plane] * SUB
        send(
            first, second, pl.ds(RENEWED_AT[plane], rows),
            state[plane, OWN_ROWS - rows :, :], state[plane, :rows, :],
        )


def middle_kernel(
    first, second, state, factor, marks, couple,
    trace_first, trace_second, kept,
    even, odd,
):
    weight = weights(couple)
    has_left, has_right = inside("xy")
    for plane in range(PLANES):
        rows = RENEWED[plane] * SUB
        at = pl.ds(RENEWED_AT[plane], rows)
        even[plane + 1, pl.ds(5 * SUB, REST), :] = jnp.zeros((REST, LANES), jnp.float32)
        even[plane + 1, pl.ds(16 * SUB, REST), :] = jnp.zeros((REST, LANES), jnp.float32)
        even[plane + 1, pl.ds(OWN_AT, OWN_ROWS), :] = state[plane]
        even[plane + 1, pl.ds(OWN_AT - rows, rows), :] = kept_if(has_left, got(first, second, at, True))
        even[plane + 1, pl.ds(16 * SUB, rows), :] = kept_if(has_right, got(first, second, at, False))
    buffers = (even, odd)
    for level in range(SIDE, STEPS):
        src, dst = buffers[level % 2], buffers[1 - level % 2]
        put_traces(src, trace_first, trace_second, level)
        keep(src, kept, LATE_KEPT, level)
        if level == STEPS - 1:
            break
        low, high = reach(level)
        ghosts(src, low + 1, high - 1)
        count = STEPS - level
        advance_groups(src, dst, factor, marks, weight, 2, count, PLANES - count, low + 1, high - 1)
        if level == SIDE:
            advance(src, dst, factor, marks, weight, 5, 2, low, high)


def second_steps(levels, buffers, kept, places, trace_first, trace_second, factor, marks, weight):
    has_below, has_above = inside("zg")
    for level in levels:
        src, dst = buffers[level % 2], buffers[1 - level % 2]
        low, high = reach(level)
        for plane in range(PLANES):
            if (level, plane) in places:
                at = span(low - 1, high + 1)
                src[plane + 1, at, :] = kept[places[level, plane], at, :]
        place = trace_place(level)
        ghosts(
            src, low, high,
            kept_if(has_below, got(trace_first, trace_second, place, True, "zg")),
            kept_if(has_above, got(trace_first, trace_second, place, False, "zg")),
        )
        groups, count, stride = (2, level + 1, 11 - level) if level < 5 else (3, 4, 4)
        advance_groups(src, dst, factor, marks, weight, groups, count, stride, low, high)


def second_kernel(
    trace_first, trace_second, kept, factor, marks, couple,
    first, second, state,
    even, odd,
):
    second_steps(range(SIDE), (even, odd), kept, EARLY_KEPT, trace_first, trace_second, factor, marks, weights(couple))
    for i, plane in enumerate(EDGE_PLANES):
        state[i] = even[plane + 1, pl.ds(OWN_AT, OWN_ROWS), :]
        send(first, second, i, state[i, HALF:, :], state[i, :HALF, :])


def last_kernel(
    trace_first, trace_second, first, second, state, kept, factor, marks, couple,
    result,
    even, odd,
):
    has_left, has_right = inside("xy")
    for i, plane in enumerate(EDGE_PLANES):
        even[plane + 1, pl.ds(OWN_AT, OWN_ROWS), :] = state[i]
        even[plane + 1, pl.ds(OWN_AT - HALF, HALF), :] = kept_if(has_left, got(first, second, i, True))
        even[plane + 1, pl.ds(OWN_AT + OWN_ROWS, HALF), :] = kept_if(has_right, got(first, second, i, False))
    second_steps(
        range(SIDE, STEPS), (even, odd), kept, LATE_KEPT, trace_first, trace_second, factor, marks,
        weights(couple),
    )
    for plane in range(PLANES):
        for chunk in range(CHUNKS):
            result[plane, :, chunk * LANES : (chunk + 1) * LANES] = even[
                plane + 1, pl.ds(OWN_AT + chunk, OWN, stride=SUB), :
            ]


def shape(*dims):
    return jax.ShapeDtypeStruct(dims, jnp.float32)


VMEM = pl.BlockSpec(memory_space=pltpu.VMEM)
HBM = pl.BlockSpec(memory_space=pltpu.HBM)
FIELD = (PLANES, ROWS * SUB, LANES)
PADDED = (PLANES + 2, ROWS * SUB, LANES)
CELLS = (PLANES, OWN_ROWS, LANES)
TRACES = (TRACE_AT[-1], LANES)
WIDE = (PLANES, OWN, CHUNKS * LANES)
PACKET = (PLANES * NEAR, LANES)
CODES = (3 * PLANES + 4, LANES)
SHARE = (RENEWED_AT[-1], LANES)
EDGE_SHARE = (len(EDGE_PLANES), HALF, LANES)


def call(kernel, outs, scratch, *operands, place=VMEM, limit=VMEM_LIMIT):
    return pl.pallas_call(
        kernel,
        out_shape=[shape(*dims) for dims in outs],
        in_specs=[place] * len(operands),
        out_specs=[VMEM] * len(outs),
        scratch_shapes=scratch,
        compiler_params=pltpu.CompilerParams(vmem_limit_bytes=limit),
        name=kernel.__name__,
    )(*operands)


def scratch(*shapes):
    return [pltpu.VMEM(dims, jnp.float32) for dims in shapes]


def swap(first, second, axis):
    levels, lines = lax.axis_size("zg"), lax.axis_size("xy")
    count = lax.axis_size(axis)

    def device(along, other):
        return along * lines + other if axis == "zg" else other * lines + along

    shifted, pairs = [], []
    for other in range(levels * lines // count):
        shifted += [(device(i, other), device(i + 1, other)) for i in range(1, count - 1, 2)]
        pairs += [(device(i, other), device(i + 1, other)) for i in range(0, count, 2)]
        idle = other ^ 1 if axis == "zg" else other ^ 4
        if idle > other:
            shifted += [(device(i, other), device(i, idle)) for i in (0, count - 1)]
    return tuple(
        lax.ppermute(cells, ("zg", "xy"), pairing + [(j, i) for i, j in pairing])
        for cells, pairing in ((first, shifted), (second, pairs))
    )


def on_device(start_field, diffusivity, tile_block, block_material, material_coupling):
    turned = jnp.swapaxes(material_coupling, 1, 2)
    empty = jnp.zeros((TILE, TILE), jnp.float32)
    couple = jnp.concatenate(
        [jnp.block([[turned[kind], empty], [empty, turned[kind]]]) for kind in (0, 1)], axis=1
    )
    material = block_material.reshape(-1, LANES)
    first, second = call(
        prepare_kernel,
        [PACKET, PACKET],
        scratch(start_field.shape, diffusivity.shape, CELLS, CELLS) + [pltpu.SemaphoreType.DMA((4,))],
        start_field, diffusivity,
        place=HBM,
        limit=PREPARE_LIMIT,
    )
    near = swap(first, second, "xy")
    first, second, code = call(
        code_kernel,
        [CODES, CODES, (PLANES, OWN, LANES)],
        [pltpu.VMEM((PLANES, OWN, LANES), jnp.int32)],
        tile_block, material,
    )
    codes = swap(first, second, "xy")
    field, conduct, code = call(
        own_kernel, [FIELD] * 3, scratch(WIDE), start_field, diffusivity, code
    )
    first, second, trace_first, trace_second, state, early_kept, factor, marks = call(
        first_kernel,
        [SHARE, SHARE, TRACES, TRACES, CELLS, (len(EARLY_KEPT), ROWS * SUB, LANES), FIELD, FIELD],
        scratch(PADDED, PADDED, WIDE, (PLANES, OWN, LANES)),
        *near, *codes, field, conduct, code, couple,
    )
    sides = swap(first, second, "xy")
    early = swap(trace_first, trace_second, "zg")
    trace_first, trace_second, late_kept = call(
        middle_kernel,
        [TRACES, TRACES, (len(LATE_KEPT), ROWS * SUB, LANES)],
        scratch(PADDED, PADDED),
        *sides, state, factor, marks, couple,
    )
    late = swap(trace_first, trace_second, "zg")
    first, second, state = call(
        second_kernel,
        [EDGE_SHARE, EDGE_SHARE, (len(EDGE_PLANES), OWN_ROWS, LANES)],
        scratch(PADDED, PADDED),
        *early, early_kept, factor, marks, couple,
    )
    sides = swap(first, second, "xy")
    (result,) = call(
        last_kernel,
        [start_field.shape],
        scratch(PADDED, PADDED),
        *late, *sides, state, late_kept, factor, marks, couple,
    )
    return result


def solution(mesh):
    return jax.shard_map(
        on_device,
        mesh=mesh,
        in_specs=(P("zg", "xy", None), P("zg", "xy", None), P("zg", "xy", None), P(), P()),
        out_specs=P("zg", "xy", None),
        check_vma=False,
    )
```

```python
import jax
import jax.numpy as jnp
from jax import lax
from jax.experimental import pallas as pl
from jax.experimental.pallas import tpu as pltpu
from jax.sharding import PartitionSpec as P

TILE = 64
STEPS = 8
PLANES = 12
OWN = 8
HALO = 8
ROWS = OWN + 2 * HALO
SUB = 8
LANES = 128
CHUNKS = 8
VMEM_LIMIT = 24 * 1024 * 1024
PREPARE_LIMIT = 53 * 1024 * 1024


SIDE = 4
OWN_AT = HALO * SUB
OWN_ROWS = OWN * SUB
HALF = SIDE * SUB
EDGE_PLANES = (0, 1, 2, 3, 8, 9, 10, 11)
REST = 3 * SUB
NEAR = HALF + REST
RENEWED = (3, 3, 2, 1, 4, 4, 4, 4, 1, 2, 3, 3)
RENEWED_AT = [SUB * sum(RENEWED[:plane]) for plane in range(PLANES + 1)]


def reach(level):
    margin = HALO - SIDE + 1 + level % SIDE
    return margin, ROWS - margin


def span(low, high):
    return pl.ds(low * SUB, (high - low) * SUB)


TRACE_AT = [0]
for _level in range(SIDE):
    _low, _high = reach(_level)
    TRACE_AT.append(TRACE_AT[-1] + (_high - _low) * SUB)


def trace_place(level):
    start = TRACE_AT[level % SIDE]
    return pl.ds(start, TRACE_AT[level % SIDE + 1] - start)


KEPT = [(level, plane) for level in range(6) for plane in sorted({level, level + 1, 10 - level, 11 - level})]
EARLY_KEPT = {pair: i for i, pair in enumerate(pair for pair in KEPT if pair[0] < SIDE)}
LATE_KEPT = {pair: i for i, pair in enumerate(pair for pair in KEPT if pair[0] >= SIDE)}


def span_sum(cells):
    lane = lax.broadcasted_iota(jnp.int32, (1, SUB, LANES), 2)
    row = lax.broadcasted_iota(jnp.int32, (1, SUB, LANES), 1)
    after = jnp.where(row == SUB - 1, 0.0, pltpu.roll(cells, SUB - 1, 1))
    before = jnp.where(row == 0, 0.0, pltpu.roll(cells, 1, 1))
    return pltpu.roll(jnp.where(lane == 0, after, cells), LANES - 1, 2) + pltpu.roll(
        jnp.where(lane == LANES - 1, before, cells), 1, 2
    )


def split_cells(values):
    high = values.astype(jnp.bfloat16)
    low = (values - high.astype(jnp.float32)).astype(jnp.bfloat16)
    return high, low


def weights(couple_ref):
    high, low = split_cells(couple_ref[...])
    return jnp.concatenate([high, high, low], axis=0)


def advance(src, dst, conduct, code, weight, first, count, low, high):
    rows = high - low
    at = pl.ds(low * SUB, rows * SUB)
    mid = pl.ds(first + 1, count)
    here = src[mid, at, :]
    around = (
        src[pl.ds(first, count), at, :]
        + src[pl.ds(first + 2, count), at, :]
        + src[mid, pl.ds((low - 1) * SUB, rows * SUB), :]
        + src[mid, pl.ds((low + 1) * SUB, rows * SUB), :]
    )
    along = span_sum(here.reshape(count * rows, SUB, LANES)).reshape(here.shape)
    flat = here.reshape(count * rows * SUB, LANES)
    near, rest = split_cells(flat)
    product = jnp.dot(
        jnp.concatenate([near, rest, near], axis=1), weight, preferred_element_type=jnp.float32
    )
    plane = pl.ds(first, count)
    marks = code[plane, at, :]
    penalty = jnp.where(
        marks == 1.0,
        product[:, :LANES].reshape(here.shape),
        jnp.where(marks == 2.0, product[:, LANES:].reshape(here.shape), 0.0),
    )
    dst[mid, at, :] = here + conduct[plane, at, :] * (around + along - 6.0 * here) - penalty


def advance_groups(src, dst, conduct, code, weight, groups, count, stride, low, high):
    for i in range(groups):
        advance(src, dst, conduct, code, weight, i * stride, count, low, high)


def inside(axis):
    place = lax.axis_index(axis)
    return place > 0, place < lax.axis_size(axis) - 1


def kept_if(flag, values):
    return jnp.where(flag, values, 0.0)


def odd_place(axis):
    return lax.axis_index(axis) % 2 == 1


def send(first, second, at, upward, downward, axis="xy"):
    odd = odd_place(axis)
    first[at] = jnp.where(odd, upward, downward)
    second[at] = jnp.where(odd, downward, upward)


def got(first, second, at, from_before, axis="xy"):
    return jnp.where(odd_place(axis) == from_before, second[at], first[at])


def spread(block, dst, offset, at_plane, planes=range(PLANES)):
    for plane in planes:
        for chunk in range(CHUNKS):
            dst[plane + at_plane, pl.ds(offset * SUB + chunk, OWN, stride=SUB), :] = block[
                plane, :, chunk * LANES : (chunk + 1) * LANES
            ]


def widened(codes):
    tile_of = lax.broadcasted_iota(jnp.int32, (LANES, CHUNKS * LANES), 0)
    cell_of = lax.broadcasted_iota(jnp.int32, (LANES, CHUNKS * LANES), 1)
    widen = jnp.where(tile_of == cell_of // TILE, 1.0, 0.0).astype(jnp.bfloat16)
    flat = codes.reshape(-1, LANES).astype(jnp.bfloat16)
    wide = jnp.dot(flat, widen, preferred_element_type=jnp.float32)
    return wide.reshape(codes.shape[0], OWN, CHUNKS * LANES)


def ghosts(src, low, high, from_below=None, from_above=None):
    at = span(low, high)
    if from_below is None:
        src[0, at, :] = src[1, at, :] * 0.6
        src[PLANES + 1, at, :] = src[PLANES, at, :] * 0.6
    else:
        src[0, at, :] = (from_below + 0.75 * src[1, at, :]) * 0.8
        src[PLANES + 1, at, :] = (from_above + 0.75 * src[PLANES, at, :]) * 0.8


def put_traces(src, first, second, level):
    at = span(*reach(level))
    place = trace_place(level)
    to_below = 0.75 * src[2, at, :] - 0.25 * src[1, at, :]
    to_above = 0.75 * src[PLANES - 1, at, :] - 0.25 * src[PLANES, at, :]
    send(first, second, place, to_above, to_below, "zg")


def prepare_kernel(start_field, diffusivity, first, second, own_v, own_d, field, conduct, arrived):
    half = PLANES // 2
    loads = []
    for part in range(2):
        at = pl.ds(part * half, half)
        for source, target in ((start_field, own_v), (diffusivity, own_d)):
            load = pltpu.make_async_copy(source.at[at], target.at[at], arrived.at[len(loads)])
            load.start()
            loads.append(load)
    for part in range(2):
        planes = range(part * half, part * half + half)
        loads[2 * part].wait()
        spread(own_v, field, 0, 0, planes)
        loads[2 * part + 1].wait()
        spread(own_d, conduct, 0, 0, planes)
        for plane in planes:
            at = plane * NEAR
            send(first, second, pl.ds(at, HALF), field[plane, HALF:, :], field[plane, :HALF, :])
            send(
                first, second, pl.ds(at + HALF, REST),
                conduct[plane, OWN_ROWS - REST :, :], conduct[plane, :REST, :],
            )


def code_kernel(tile_block, material, first, second, code, tiles):
    tiles[...] = jnp.zeros(tiles.shape, jnp.int32)
    tiles[:, :, : tile_block.shape[2]] = tile_block[...]
    table = material[...]
    row = lax.broadcasted_iota(jnp.int32, (SUB, LANES), 0)
    bits = jnp.zeros((SUB, LANES), jnp.int32)
    for part in range(table.shape[0] // SUB):
        bits = bits + (table[part * SUB : (part + 1) * SUB] << (row + part * SUB))
    for shift in (4, 2, 1):
        bits = bits + pltpu.roll(bits, shift, 0)
    for plane in range(PLANES):
        block = tiles[plane]
        entry = jnp.maximum(block - 1, 0)
        word = jnp.take_along_axis(bits, entry & (LANES - 1), axis=1)
        kind = (word >> (entry >> 7)) & 1
        code[plane] = jnp.where(block > 0, kind + 1, 0).astype(jnp.float32)
        send(first, second, pl.ds(3 * plane, 3), code[plane, 5:, :], code[plane, :3, :])
    for packet in (first, second):
        packet[3 * PLANES :, :] = jnp.zeros((4, LANES), jnp.float32)


def own_kernel(
    start_field, diffusivity, code, couple,
    field, factor, marks, inner_1, inner_2, inner_3,
    even, odd, wide,
):
    own = pl.ds(OWN_AT, OWN_ROWS)
    spread(start_field, even, HALO, 1)
    spread(diffusivity, factor, HALO, 0)
    wide[...] = widened(code[...])
    spread(wide, marks, HALO, 0)
    field[...] = even[1 : PLANES + 1, own, :]
    weight = weights(couple)
    buffers = (even, odd)
    for level, inner in enumerate((inner_1, inner_2, inner_3)):
        src, dst = buffers[level % 2], buffers[1 - level % 2]
        low, high = HALO + 1 + level, HALO + OWN - 1 - level
        ghosts(src, low, high)
        advance(src, dst, factor, marks, weight, 0, PLANES, low, high)
        inner[...] = dst[1 : PLANES + 1, span(low, high), :]


def keep(src, kept, places, level):
    low, high = reach(level)
    at = span(low - 1, high + 1)
    for plane in range(PLANES):
        if (level, plane) in places:
            kept[places[level, plane], at, :] = src[plane + 1, at, :]


def first_kernel(
    near_first, near_second, code_first, code_second,
    field, conduct, code, inner_1, inner_2, inner_3, couple,
    first, second, trace_first, trace_second, state, kept, factor, marks,
    even, odd, wide, codes,
):
    weight = weights(couple)
    has_left, has_right = inside("xy")
    own = pl.ds(OWN_AT, OWN_ROWS)
    for flag, from_left, offset, near_at, rest_at, place in (
        (has_left, True, 0, 4 * SUB, 5 * SUB, 5),
        (has_right, False, HALO + OWN, 16 * SUB, 16 * SUB, 0),
    ):
        def packet(at, size):
            return kept_if(flag, got(near_first, near_second, pl.ds(at, size), from_left))

        codes[...] = jnp.zeros(codes.shape, jnp.float32)
        for plane in range(PLANES):
            at = plane * NEAR
            even[plane + 1, pl.ds(near_at, HALF), :] = packet(at, HALF)
            factor[plane, pl.ds(rest_at, REST), :] = packet(at + HALF, REST)
            codes[plane, place : place + 3, :] = kept_if(
                flag, got(code_first, code_second, pl.ds(3 * plane, 3), from_left)
            )
        wide[...] = widened(codes[...])
        spread(wide, marks, offset, 0)
    even[1 : PLANES + 1, own, :] = field[...]
    factor[:, own, :] = conduct[:, own, :]
    marks[:, own, :] = code[:, own, :]
    buffers = (even, odd)
    for level in range(SIDE):
        src, dst = buffers[level % 2], buffers[1 - level % 2]
        put_traces(src, trace_first, trace_second, level)
        keep(src, kept, EARLY_KEPT, level)
        low, high = reach(level)
        ghosts(src, low, high)
        for outer in (low, high - SIDE):
            advance(src, dst, factor, marks, weight, 0, PLANES, outer, outer + SIDE)
        if level < SIDE - 1:
            inner = (inner_1, inner_2, inner_3)[level]
            dst[1 : PLANES + 1, span(low + SIDE, high - SIDE), :] = inner[...]
    state[...] = even[1 : PLANES + 1, OWN_AT : OWN_AT + OWN_ROWS, :]
    for plane in range(PLANES):
        rows = RENEWED[plane] * SUB
        send(
            first, second, pl.ds(RENEWED_AT[plane], rows),
            state[plane, OWN_ROWS - rows :, :], state[plane, :rows, :],
        )


def middle_kernel(
    first, second, state, factor, marks, couple,
    trace_first, trace_second, kept,
    even, odd,
):
    weight = weights(couple)
    has_left, has_right = inside("xy")
    for plane in range(PLANES):
        rows = RENEWED[plane] * SUB
        at = pl.ds(RENEWED_AT[plane], rows)
        even[plane + 1, pl.ds(5 * SUB, REST), :] = jnp.zeros((REST, LANES), jnp.float32)
        even[plane + 1, pl.ds(16 * SUB, REST), :] = jnp.zeros((REST, LANES), jnp.float32)
        even[plane + 1, pl.ds(OWN_AT, OWN_ROWS), :] = state[plane]
        even[plane + 1, pl.ds(OWN_AT - rows, rows), :] = kept_if(has_left, got(first, second, at, True))
        even[plane + 1, pl.ds(16 * SUB, rows), :] = kept_if(has_right, got(first, second, at, False))
    buffers = (even, odd)
    for level in range(SIDE, STEPS):
        src, dst = buffers[level % 2], buffers[1 - level % 2]
        put_traces(src, trace_first, trace_second, level)
        keep(src, kept, LATE_KEPT, level)
        if level == STEPS - 1:
            break
        low, high = reach(level)
        ghosts(src, low + 1, high - 1)
        count = STEPS - level
        advance_groups(src, dst, factor, marks, weight, 2, count, PLANES - count, low + 1, high - 1)
        if level == SIDE:
            advance(src, dst, factor, marks, weight, 5, 2, low, high)


def second_steps(levels, buffers, kept, places, trace_first, trace_second, factor, marks, weight):
    has_below, has_above = inside("zg")
    for level in levels:
        src, dst = buffers[level % 2], buffers[1 - level % 2]
        low, high = reach(level)
        for plane in range(PLANES):
            if (level, plane) in places:
                at = span(low - 1, high + 1)
                src[plane + 1, at, :] = kept[places[level, plane], at, :]
        place = trace_place(level)
        ghosts(
            src, low, high,
            kept_if(has_below, got(trace_first, trace_second, place, True, "zg")),
            kept_if(has_above, got(trace_first, trace_second, place, False, "zg")),
        )
        groups, count, stride = (2, level + 1, 11 - level) if level < 5 else (3, 4, 4)
        advance_groups(src, dst, factor, marks, weight, groups, count, stride, low, high)


def second_kernel(
    trace_first, trace_second, kept, factor, marks, couple,
    first, second, state,
    even, odd,
):
    second_steps(range(SIDE), (even, odd), kept, EARLY_KEPT, trace_first, trace_second, factor, marks, weights(couple))
    for i, plane in enumerate(EDGE_PLANES):
        state[i] = even[plane + 1, pl.ds(OWN_AT, OWN_ROWS), :]
        send(first, second, i, state[i, HALF:, :], state[i, :HALF, :])


def last_kernel(
    trace_first, trace_second, first, second, state, kept, factor, marks, couple,
    result,
    even, odd,
):
    has_left, has_right = inside("xy")
    for i, plane in enumerate(EDGE_PLANES):
        even[plane + 1, pl.ds(OWN_AT, OWN_ROWS), :] = state[i]
        even[plane + 1, pl.ds(OWN_AT - HALF, HALF), :] = kept_if(has_left, got(first, second, i, True))
        even[plane + 1, pl.ds(OWN_AT + OWN_ROWS, HALF), :] = kept_if(has_right, got(first, second, i, False))
    second_steps(
        range(SIDE, STEPS), (even, odd), kept, LATE_KEPT, trace_first, trace_second, factor, marks,
        weights(couple),
    )
    for plane in range(PLANES):
        for chunk in range(CHUNKS):
            result[plane, :, chunk * LANES : (chunk + 1) * LANES] = even[
                plane + 1, pl.ds(OWN_AT + chunk, OWN, stride=SUB), :
            ]


def shape(*dims):
    return jax.ShapeDtypeStruct(dims, jnp.float32)


VMEM = pl.BlockSpec(memory_space=pltpu.VMEM)
HBM = pl.BlockSpec(memory_space=pltpu.HBM)
FIELD = (PLANES, ROWS * SUB, LANES)
PADDED = (PLANES + 2, ROWS * SUB, LANES)
CELLS = (PLANES, OWN_ROWS, LANES)
TRACES = (TRACE_AT[-1], LANES)
WIDE = (PLANES, OWN, CHUNKS * LANES)
PACKET = (PLANES * NEAR, LANES)
CODES = (3 * PLANES + 4, LANES)
SHARE = (RENEWED_AT[-1], LANES)
EDGE_SHARE = (len(EDGE_PLANES), HALF, LANES)


def call(kernel, outs, scratch, *operands, place=VMEM, limit=VMEM_LIMIT):
    return pl.pallas_call(
        kernel,
        out_shape=[shape(*dims) for dims in outs],
        in_specs=[place] * len(operands),
        out_specs=[VMEM] * len(outs),
        scratch_shapes=scratch,
        compiler_params=pltpu.CompilerParams(vmem_limit_bytes=limit),
        name=kernel.__name__,
    )(*operands)


def scratch(*shapes):
    return [pltpu.VMEM(dims, jnp.float32) for dims in shapes]


def swap(first, second, axis):
    levels, lines = lax.axis_size("zg"), lax.axis_size("xy")
    count = lax.axis_size(axis)

    def device(along, other):
        return along * lines + other if axis == "zg" else other * lines + along

    shifted, pairs = [], []
    for other in range(levels * lines // count):
        shifted += [(device(i, other), device(i + 1, other)) for i in range(1, count - 1, 2)]
        pairs += [(device(i, other), device(i + 1, other)) for i in range(0, count, 2)]
        idle = other ^ 1 if axis == "zg" else other ^ 4
        if idle > other:
            shifted += [(device(i, other), device(i, idle)) for i in (0, count - 1)]
    return tuple(
        lax.ppermute(cells, ("zg", "xy"), pairing + [(j, i) for i, j in pairing])
        for cells, pairing in ((first, shifted), (second, pairs))
    )


def on_device(start_field, diffusivity, tile_block, block_material, material_coupling):
    turned = jnp.swapaxes(material_coupling, 1, 2)
    empty = jnp.zeros((TILE, TILE), jnp.float32)
    couple = jnp.concatenate(
        [jnp.block([[turned[kind], empty], [empty, turned[kind]]]) for kind in (0, 1)], axis=1
    )
    material = block_material.reshape(-1, LANES)
    first, second = call(
        prepare_kernel,
        [PACKET, PACKET],
        scratch(start_field.shape, diffusivity.shape, CELLS, CELLS) + [pltpu.SemaphoreType.DMA((4,))],
        start_field, diffusivity,
        place=HBM,
        limit=PREPARE_LIMIT,
    )
    near = swap(first, second, "xy")
    first, second, code = call(
        code_kernel,
        [CODES, CODES, (PLANES, OWN, LANES)],
        [pltpu.VMEM((PLANES, OWN, LANES), jnp.int32)],
        tile_block, material,
    )
    codes = swap(first, second, "xy")
    field, conduct, code, *inner = call(
        own_kernel,
        [CELLS, FIELD, FIELD] + [(PLANES, (OWN - 2 * level) * SUB, LANES) for level in (1, 2, 3)],
        scratch(PADDED, PADDED, WIDE),
        start_field, diffusivity, code, couple,
    )
    first, second, trace_first, trace_second, state, early_kept, factor, marks = call(
        first_kernel,
        [SHARE, SHARE, TRACES, TRACES, CELLS, (len(EARLY_KEPT), ROWS * SUB, LANES), FIELD, FIELD],
        scratch(PADDED, PADDED, WIDE, (PLANES, OWN, LANES)),
        *near, *codes, field, conduct, code, *inner, couple,
    )
    sides = swap(first, second, "xy")
    early = swap(trace_first, trace_second, "zg")
    trace_first, trace_second, late_kept = call(
        middle_kernel,
        [TRACES, TRACES, (len(LATE_KEPT), ROWS * SUB, LANES)],
        scratch(PADDED, PADDED),
        *sides, state, factor, marks, couple,
    )
    late = swap(trace_first, trace_second, "zg")
    first, second, state = call(
        second_kernel,
        [EDGE_SHARE, EDGE_SHARE, (len(EDGE_PLANES), OWN_ROWS, LANES)],
        scratch(PADDED, PADDED),
        *early, early_kept, factor, marks, couple,
    )
    sides = swap(first, second, "xy")
    (result,) = call(
        last_kernel,
        [start_field.shape],
        scratch(PADDED, PADDED),
        *late, *sides, state, late_kept, factor, marks, couple,
    )
    return result


def solution(mesh):
    return jax.shard_map(
        on_device,
        mesh=mesh,
        in_specs=(P("zg", "xy", None), P("zg", "xy", None), P("zg", "xy", None), P(), P()),
        out_specs=P("zg", "xy", None),
        check_vma=False,
    )
```

```python
import jax
import jax.numpy as jnp
from jax import lax
from jax.experimental import pallas as pl
from jax.experimental.pallas import tpu as pltpu
from jax.sharding import PartitionSpec as P

TILE = 64
STEPS = 8
PLANES = 12
OWN = 8
HALO = 8
ROWS = OWN + 2 * HALO
SUB = 8
LANES = 128
CHUNKS = 8
VMEM_LIMIT = 24 * 1024 * 1024
PREPARE_LIMIT = 53 * 1024 * 1024


SIDE = 4
OWN_AT = HALO * SUB
OWN_ROWS = OWN * SUB
HALF = SIDE * SUB
EDGE_PLANES = (0, 1, 2, 3, 8, 9, 10, 11)
REST = 3 * SUB
NEAR = HALF + REST
RENEWED = (3, 3, 2, 1, 4, 4, 4, 4, 1, 2, 3, 3)
RENEWED_AT = [SUB * sum(RENEWED[:plane]) for plane in range(PLANES + 1)]


def reach(level):
    margin = HALO - SIDE + 1 + level % SIDE
    return margin, ROWS - margin


def span(low, high):
    return pl.ds(low * SUB, (high - low) * SUB)


TRACE_AT = [0]
for _level in range(SIDE):
    _low, _high = reach(_level)
    TRACE_AT.append(TRACE_AT[-1] + (_high - _low) * SUB)


def trace_place(level):
    start = TRACE_AT[level % SIDE]
    return pl.ds(start, TRACE_AT[level % SIDE + 1] - start)


KEPT = [(level, plane) for level in range(6) for plane in sorted({level, level + 1, 10 - level, 11 - level})]
EARLY_KEPT = {pair: i for i, pair in enumerate(pair for pair in KEPT if pair[0] < SIDE)}
LATE_KEPT = {pair: i for i, pair in enumerate(pair for pair in KEPT if pair[0] >= SIDE)}


def span_sum(cells):
    lane = lax.broadcasted_iota(jnp.int32, (1, SUB, LANES), 2)
    row = lax.broadcasted_iota(jnp.int32, (1, SUB, LANES), 1)
    after = jnp.where(row == SUB - 1, 0.0, pltpu.roll(cells, SUB - 1, 1))
    before = jnp.where(row == 0, 0.0, pltpu.roll(cells, 1, 1))
    return pltpu.roll(jnp.where(lane == 0, after, cells), LANES - 1, 2) + pltpu.roll(
        jnp.where(lane == LANES - 1, before, cells), 1, 2
    )


def split_cells(values):
    high = values.astype(jnp.bfloat16)
    low = (values - high.astype(jnp.float32)).astype(jnp.bfloat16)
    return high, low


def weights(couple_ref):
    high, low = split_cells(couple_ref[...])
    return jnp.concatenate([high, high, low], axis=0)


def advance(src, dst, conduct, code, weight, first, count, low, high):
    rows = high - low
    at = pl.ds(low * SUB, rows * SUB)
    mid = pl.ds(first + 1, count)
    here = src[mid, at, :]
    around = (
        src[pl.ds(first, count), at, :]
        + src[pl.ds(first + 2, count), at, :]
        + src[mid, pl.ds((low - 1) * SUB, rows * SUB), :]
        + src[mid, pl.ds((low + 1) * SUB, rows * SUB), :]
    )
    along = span_sum(here.reshape(count * rows, SUB, LANES)).reshape(here.shape)
    flat = here.reshape(count * rows * SUB, LANES)
    near, rest = split_cells(flat)
    product = jnp.dot(
        jnp.concatenate([near, rest, near], axis=1), weight, preferred_element_type=jnp.float32
    )
    plane = pl.ds(first, count)
    marks = code[plane, at, :]
    penalty = jnp.where(
        marks == 1.0,
        product[:, :LANES].reshape(here.shape),
        jnp.where(marks == 2.0, product[:, LANES:].reshape(here.shape), 0.0),
    )
    dst[mid, at, :] = here + conduct[plane, at, :] * (around + along - 6.0 * here) - penalty


def advance_groups(src, dst, conduct, code, weight, groups, count, stride, low, high):
    for i in range(groups):
        advance(src, dst, conduct, code, weight, i * stride, count, low, high)


def inside(axis):
    place = lax.axis_index(axis)
    return place > 0, place < lax.axis_size(axis) - 1


def kept_if(flag, values):
    return jnp.where(flag, values, 0.0)


def odd_place(axis):
    return lax.axis_index(axis) % 2 == 1


def send(first, second, at, upward, downward, axis="xy"):
    odd = odd_place(axis)
    first[at] = jnp.where(odd, upward, downward)
    second[at] = jnp.where(odd, downward, upward)


def got(first, second, at, from_before, axis="xy"):
    return jnp.where(odd_place(axis) == from_before, second[at], first[at])


def spread(block, dst, offset, at_plane, planes=range(PLANES)):
    for plane in planes:
        for chunk in range(CHUNKS):
            dst[plane + at_plane, pl.ds(offset * SUB + chunk, OWN, stride=SUB), :] = block[
                plane, :, chunk * LANES : (chunk + 1) * LANES
            ]


def widened(codes):
    tile_of = lax.broadcasted_iota(jnp.int32, (LANES, CHUNKS * LANES), 0)
    cell_of = lax.broadcasted_iota(jnp.int32, (LANES, CHUNKS * LANES), 1)
    widen = jnp.where(tile_of == cell_of // TILE, 1.0, 0.0).astype(jnp.bfloat16)
    flat = codes.reshape(-1, LANES).astype(jnp.bfloat16)
    wide = jnp.dot(flat, widen, preferred_element_type=jnp.float32)
    return wide.reshape(codes.shape[0], OWN, CHUNKS * LANES)


def ghosts(src, low, high, from_below=None, from_above=None):
    at = span(low, high)
    if from_below is None:
        src[0, at, :] = src[1, at, :] * 0.6
        src[PLANES + 1, at, :] = src[PLANES, at, :] * 0.6
    else:
        src[0, at, :] = (from_below + 0.75 * src[1, at, :]) * 0.8
        src[PLANES + 1, at, :] = (from_above + 0.75 * src[PLANES, at, :]) * 0.8


def put_traces(src, first, second, level):
    at = span(*reach(level))
    place = trace_place(level)
    to_below = 0.75 * src[2, at, :] - 0.25 * src[1, at, :]
    to_above = 0.75 * src[PLANES - 1, at, :] - 0.25 * src[PLANES, at, :]
    send(first, second, place, to_above, to_below, "zg")


def prepare_kernel(start_field, diffusivity, first, second, own_v, own_d, field, conduct, arrived):
    half = PLANES // 2
    loads = []
    for part in range(2):
        at = pl.ds(part * half, half)
        for source, target in ((start_field, own_v), (diffusivity, own_d)):
            load = pltpu.make_async_copy(source.at[at], target.at[at], arrived.at[len(loads)])
            load.start()
            loads.append(load)
    for part in range(2):
        planes = range(part * half, part * half + half)
        loads[2 * part].wait()
        spread(own_v, field, 0, 0, planes)
        loads[2 * part + 1].wait()
        spread(own_d, conduct, 0, 0, planes)
        for plane in planes:
            at = plane * NEAR
            send(first, second, pl.ds(at, HALF), field[plane, HALF:, :], field[plane, :HALF, :])
            send(
                first, second, pl.ds(at + HALF, REST),
                conduct[plane, OWN_ROWS - REST :, :], conduct[plane, :REST, :],
            )


def code_kernel(tile_block, material, first, second, code, tiles):
    tiles[...] = jnp.zeros(tiles.shape, jnp.int32)
    tiles[:, :, : tile_block.shape[2]] = tile_block[...]
    table = material[...]
    row = lax.broadcasted_iota(jnp.int32, (SUB, LANES), 0)
    bits = jnp.zeros((SUB, LANES), jnp.int32)
    for part in range(table.shape[0] // SUB):
        bits = bits + (table[part * SUB : (part + 1) * SUB] << (row + part * SUB))
    for shift in (4, 2, 1):
        bits = bits + pltpu.roll(bits, shift, 0)
    for plane in range(PLANES):
        block = tiles[plane]
        entry = jnp.maximum(block - 1, 0)
        word = jnp.take_along_axis(bits, entry & (LANES - 1), axis=1)
        kind = (word >> (entry >> 7)) & 1
        code[plane] = jnp.where(block > 0, kind + 1, 0).astype(jnp.float32)
        send(first, second, pl.ds(3 * plane, 3), code[plane, 5:, :], code[plane, :3, :])
    for packet in (first, second):
        packet[3 * PLANES :, :] = jnp.zeros((4, LANES), jnp.float32)


def own_kernel(
    start_field, diffusivity, code, couple,
    field, factor, marks, inner_1, inner_2, inner_3,
    even, odd, wide,
):
    own = pl.ds(OWN_AT, OWN_ROWS)
    spread(start_field, even, HALO, 1)
    spread(diffusivity, factor, HALO, 0)
    wide[...] = widened(code[...])
    spread(wide, marks, HALO, 0)
    field[...] = even[1 : PLANES + 1, own, :]
    weight = weights(couple)
    buffers = (even, odd)
    for level, inner in enumerate((inner_1, inner_2, inner_3)):
        src, dst = buffers[level % 2], buffers[1 - level % 2]
        low, high = HALO + 1 + level, HALO + OWN - 1 - level
        ghosts(src, low, high)
        advance(src, dst, factor, marks, weight, 0, PLANES, low, high)
        inner[...] = dst[1 : PLANES + 1, span(low, high), :]


def keep(src, kept, places, level):
    low, high = reach(level)
    at = span(low - 1, high + 1)
    for plane in range(PLANES):
        if (level, plane) in places:
            kept[places[level, plane], at, :] = src[plane + 1, at, :]


def first_kernel(
    near_first, near_second, code_first, code_second,
    field, conduct, code, inner_1, inner_2, inner_3, couple,
    first, second, trace_first, trace_second, state, kept, factor, marks,
    even, odd, wide, codes,
):
    weight = weights(couple)
    has_left, has_right = inside("xy")
    own = pl.ds(OWN_AT, OWN_ROWS)
    for flag, from_left, offset, near_at, rest_at, place in (
        (has_left, True, 0, 4 * SUB, 5 * SUB, 5),
        (has_right, False, HALO + OWN, 16 * SUB, 16 * SUB, 0),
    ):
        def packet(at, size):
            return kept_if(flag, got(near_first, near_second, pl.ds(at, size), from_left))

        codes[...] = jnp.zeros(codes.shape, jnp.float32)
        for plane in range(PLANES):
            at = plane * NEAR
            even[plane + 1, pl.ds(near_at, HALF), :] = packet(at, HALF)
            factor[plane, pl.ds(rest_at, REST), :] = packet(at + HALF, REST)
            codes[plane, place : place + 3, :] = kept_if(
                flag, got(code_first, code_second, pl.ds(3 * plane, 3), from_left)
            )
        wide[...] = widened(codes[...])
        spread(wide, marks, offset, 0)
    even[1 : PLANES + 1, own, :] = field[...]
    factor[:, own, :] = conduct[:, own, :]
    marks[:, own, :] = code[:, own, :]
    buffers = (even, odd)
    for level in range(SIDE):
        src, dst = buffers[level % 2], buffers[1 - level % 2]
        put_traces(src, trace_first, trace_second, level)
        keep(src, kept, EARLY_KEPT, level)
        low, high = reach(level)
        ghosts(src, low, high)
        for outer in (low, high - SIDE):
            advance(src, dst, factor, marks, weight, 0, PLANES, outer, outer + SIDE)
        if level < SIDE - 1:
            inner = (inner_1, inner_2, inner_3)[level]
            dst[1 : PLANES + 1, span(low + SIDE, high - SIDE), :] = inner[...]
    state[...] = even[1 : PLANES + 1, OWN_AT : OWN_AT + OWN_ROWS, :]
    for plane in range(PLANES):
        rows = RENEWED[plane] * SUB
        send(
            first, second, pl.ds(RENEWED_AT[plane], rows),
            state[plane, OWN_ROWS - rows :, :], state[plane, :rows, :],
        )


def inner_kernel(state, factor, marks, couple, inner_1, inner_2, inner_3, even, odd):
    weight = weights(couple)
    even[1 : PLANES + 1, pl.ds(OWN_AT, OWN_ROWS), :] = state[...]
    buffers = (even, odd)
    for step, inner in enumerate((inner_1, inner_2, inner_3)):
        src, dst = buffers[step % 2], buffers[1 - step % 2]
        low, high = HALO + 1 + step, HALO + OWN - 1 - step
        ghosts(src, low, high)
        groups, count, stride = ((3, 4, 4), (2, 3, 9), (2, 2, 10))[step]
        advance_groups(src, dst, factor, marks, weight, groups, count, stride, low, high)
        for i in range(groups):
            plane = i * stride
            inner[plane : plane + count] = dst[plane + 1 : plane + 1 + count, span(low, high), :]


def middle_kernel(
    first, second, state, inner_1, inner_2, inner_3, factor, marks, couple,
    trace_first, trace_second, kept,
    even, odd,
):
    weight = weights(couple)
    has_left, has_right = inside("xy")
    for plane in range(PLANES):
        rows = RENEWED[plane] * SUB
        at = pl.ds(RENEWED_AT[plane], rows)
        even[plane + 1, pl.ds(5 * SUB, REST), :] = jnp.zeros((REST, LANES), jnp.float32)
        even[plane + 1, pl.ds(16 * SUB, REST), :] = jnp.zeros((REST, LANES), jnp.float32)
        even[plane + 1, pl.ds(OWN_AT, OWN_ROWS), :] = state[plane]
        even[plane + 1, pl.ds(OWN_AT - rows, rows), :] = kept_if(has_left, got(first, second, at, True))
        even[plane + 1, pl.ds(16 * SUB, rows), :] = kept_if(has_right, got(first, second, at, False))
    buffers = (even, odd)
    for level in range(SIDE, STEPS):
        src, dst = buffers[level % 2], buffers[1 - level % 2]
        put_traces(src, trace_first, trace_second, level)
        keep(src, kept, LATE_KEPT, level)
        if level == STEPS - 1:
            break
        low, high = reach(level)
        ghosts(src, low + 1, high - 1)
        count = STEPS - level
        inner = (inner_1, inner_2, inner_3)[level - SIDE]
        for outer in (low + 1, high - SIDE):
            advance_groups(src, dst, factor, marks, weight, 2, count, PLANES - count, outer, outer + 3)
        parts = [(0, count), (PLANES - count, count)]
        if level == SIDE:
            for outer in (low, high - SIDE):
                advance(src, dst, factor, marks, weight, 5, 2, outer, outer + SIDE)
            parts.append((5, 2))
        for plane, size in parts:
            dst[plane + 1 : plane + 1 + size, span(low + SIDE, high - SIDE), :] = inner[plane : plane + size]


def second_steps(levels, buffers, kept, places, trace_first, trace_second, factor, marks, weight):
    has_below, has_above = inside("zg")
    for level in levels:
        src, dst = buffers[level % 2], buffers[1 - level % 2]
        low, high = reach(level)
        for plane in range(PLANES):
            if (level, plane) in places:
                at = span(low - 1, high + 1)
                src[plane + 1, at, :] = kept[places[level, plane], at, :]
        place = trace_place(level)
        ghosts(
            src, low, high,
            kept_if(has_below, got(trace_first, trace_second, place, True, "zg")),
            kept_if(has_above, got(trace_first, trace_second, place, False, "zg")),
        )
        groups, count, stride = (2, level + 1, 11 - level) if level < 5 else (3, 4, 4)
        advance_groups(src, dst, factor, marks, weight, groups, count, stride, low, high)


def second_kernel(
    trace_first, trace_second, kept, factor, marks, couple,
    first, second, state,
    even, odd,
):
    second_steps(range(SIDE), (even, odd), kept, EARLY_KEPT, trace_first, trace_second, factor, marks, weights(couple))
    for i, plane in enumerate(EDGE_PLANES):
        state[i] = even[plane + 1, pl.ds(OWN_AT, OWN_ROWS), :]
        send(first, second, i, state[i, HALF:, :], state[i, :HALF, :])


def last_kernel(
    trace_first, trace_second, first, second, state, kept, factor, marks, couple,
    result,
    even, odd,
):
    has_left, has_right = inside("xy")
    for i, plane in enumerate(EDGE_PLANES):
        even[plane + 1, pl.ds(OWN_AT, OWN_ROWS), :] = state[i]
        even[plane + 1, pl.ds(OWN_AT - HALF, HALF), :] = kept_if(has_left, got(first, second, i, True))
        even[plane + 1, pl.ds(OWN_AT + OWN_ROWS, HALF), :] = kept_if(has_right, got(first, second, i, False))
    second_steps(
        range(SIDE, STEPS), (even, odd), kept, LATE_KEPT, trace_first, trace_second, factor, marks,
        weights(couple),
    )
    for plane in range(PLANES):
        for chunk in range(CHUNKS):
            result[plane, :, chunk * LANES : (chunk + 1) * LANES] = even[
                plane + 1, pl.ds(OWN_AT + chunk, OWN, stride=SUB), :
            ]


def shape(*dims):
    return jax.ShapeDtypeStruct(dims, jnp.float32)


VMEM = pl.BlockSpec(memory_space=pltpu.VMEM)
HBM = pl.BlockSpec(memory_space=pltpu.HBM)
FIELD = (PLANES, ROWS * SUB, LANES)
PADDED = (PLANES + 2, ROWS * SUB, LANES)
CELLS = (PLANES, OWN_ROWS, LANES)
TRACES = (TRACE_AT[-1], LANES)
WIDE = (PLANES, OWN, CHUNKS * LANES)
PACKET = (PLANES * NEAR, LANES)
CODES = (3 * PLANES + 4, LANES)
SHARE = (RENEWED_AT[-1], LANES)
EDGE_SHARE = (len(EDGE_PLANES), HALF, LANES)


def call(kernel, outs, scratch, *operands, place=VMEM, limit=VMEM_LIMIT):
    return pl.pallas_call(
        kernel,
        out_shape=[shape(*dims) for dims in outs],
        in_specs=[place] * len(operands),
        out_specs=[VMEM] * len(outs),
        scratch_shapes=scratch,
        compiler_params=pltpu.CompilerParams(vmem_limit_bytes=limit),
        name=kernel.__name__,
    )(*operands)


def scratch(*shapes):
    return [pltpu.VMEM(dims, jnp.float32) for dims in shapes]


def swap(first, second, axis):
    levels, lines = lax.axis_size("zg"), lax.axis_size("xy")
    count = lax.axis_size(axis)

    def device(along, other):
        return along * lines + other if axis == "zg" else other * lines + along

    shifted, pairs = [], []
    for other in range(levels * lines // count):
        shifted += [(device(i, other), device(i + 1, other)) for i in range(1, count - 1, 2)]
        pairs += [(device(i, other), device(i + 1, other)) for i in range(0, count, 2)]
        idle = other ^ 1 if axis == "zg" else other ^ 4
        if idle > other:
            shifted += [(device(i, other), device(i, idle)) for i in (0, count - 1)]
    return tuple(
        lax.ppermute(cells, ("zg", "xy"), pairing + [(j, i) for i, j in pairing])
        for cells, pairing in ((first, shifted), (second, pairs))
    )


def on_device(start_field, diffusivity, tile_block, block_material, material_coupling):
    turned = jnp.swapaxes(material_coupling, 1, 2)
    empty = jnp.zeros((TILE, TILE), jnp.float32)
    couple = jnp.concatenate(
        [jnp.block([[turned[kind], empty], [empty, turned[kind]]]) for kind in (0, 1)], axis=1
    )
    material = block_material.reshape(-1, LANES)
    first, second = call(
        prepare_kernel,
        [PACKET, PACKET],
        scratch(start_field.shape, diffusivity.shape, CELLS, CELLS) + [pltpu.SemaphoreType.DMA((4,))],
        start_field, diffusivity,
        place=HBM,
        limit=PREPARE_LIMIT,
    )
    near = swap(first, second, "xy")
    first, second, code = call(
        code_kernel,
        [CODES, CODES, (PLANES, OWN, LANES)],
        [pltpu.VMEM((PLANES, OWN, LANES), jnp.int32)],
        tile_block, material,
    )
    codes = swap(first, second, "xy")
    field, conduct, code, *inner = call(
        own_kernel,
        [CELLS, FIELD, FIELD] + [(PLANES, (OWN - 2 * level) * SUB, LANES) for level in (1, 2, 3)],
        scratch(PADDED, PADDED, WIDE),
        start_field, diffusivity, code, couple,
    )
    first, second, trace_first, trace_second, state, early_kept, factor, marks = call(
        first_kernel,
        [SHARE, SHARE, TRACES, TRACES, CELLS, (len(EARLY_KEPT), ROWS * SUB, LANES), FIELD, FIELD],
        scratch(PADDED, PADDED, WIDE, (PLANES, OWN, LANES)),
        *near, *codes, field, conduct, code, *inner, couple,
    )
    sides = swap(first, second, "xy")
    early = swap(trace_first, trace_second, "zg")
    inner = call(
        inner_kernel,
        [(PLANES, (OWN - 2 * step) * SUB, LANES) for step in (1, 2, 3)],
        scratch(PADDED, PADDED),
        state, factor, marks, couple,
    )
    trace_first, trace_second, late_kept = call(
        middle_kernel,
        [TRACES, TRACES, (len(LATE_KEPT), ROWS * SUB, LANES)],
        scratch(PADDED, PADDED),
        *sides, state, *inner, factor, marks, couple,
    )
    late = swap(trace_first, trace_second, "zg")
    first, second, state = call(
        second_kernel,
        [EDGE_SHARE, EDGE_SHARE, (len(EDGE_PLANES), OWN_ROWS, LANES)],
        scratch(PADDED, PADDED),
        *early, early_kept, factor, marks, couple,
    )
    sides = swap(first, second, "xy")
    (result,) = call(
        last_kernel,
        [start_field.shape],
        scratch(PADDED, PADDED),
        *late, *sides, state, late_kept, factor, marks, couple,
    )
    return result


def solution(mesh):
    return jax.shard_map(
        on_device,
        mesh=mesh,
        in_specs=(P("zg", "xy", None), P("zg", "xy", None), P("zg", "xy", None), P(), P()),
        out_specs=P("zg", "xy", None),
        check_vma=False,
    )
```

```python
import jax
import jax.numpy as jnp
from jax import lax
from jax.experimental import pallas as pl
from jax.experimental.pallas import tpu as pltpu
from jax.sharding import PartitionSpec as P

TILE = 64
STEPS = 8
PLANES = 12
OWN = 8
HALO = 8
ROWS = OWN + 2 * HALO
SUB = 8
LANES = 128
CHUNKS = 8
VMEM_LIMIT = 24 * 1024 * 1024
PREPARE_LIMIT = 53 * 1024 * 1024


SIDE = 4
OWN_AT = HALO * SUB
OWN_ROWS = OWN * SUB
HALF = SIDE * SUB
EDGE_PLANES = (0, 1, 2, 3, 8, 9, 10, 11)
REST = 3 * SUB
NEAR = HALF + REST
RENEWED = (3, 3, 2, 1, 4, 4, 4, 4, 1, 2, 3, 3)
RENEWED_AT = [SUB * sum(RENEWED[:plane]) for plane in range(PLANES + 1)]


def reach(level):
    margin = HALO - SIDE + 1 + level % SIDE
    return margin, ROWS - margin


def span(low, high):
    return pl.ds(low * SUB, (high - low) * SUB)


TRACE_AT = [0]
for _level in range(SIDE):
    _low, _high = reach(_level)
    TRACE_AT.append(TRACE_AT[-1] + (_high - _low) * SUB)


def trace_place(level):
    start = TRACE_AT[level % SIDE]
    return pl.ds(start, TRACE_AT[level % SIDE + 1] - start)


KEPT = [(level, plane) for level in range(6) for plane in sorted({level, level + 1, 10 - level, 11 - level})]
EARLY_KEPT = {pair: i for i, pair in enumerate(pair for pair in KEPT if pair[0] < SIDE)}
LATE_KEPT = {pair: i for i, pair in enumerate(pair for pair in KEPT if pair[0] >= SIDE)}


def span_sum(cells):
    lane = lax.broadcasted_iota(jnp.int32, (1, SUB, LANES), 2)
    row = lax.broadcasted_iota(jnp.int32, (1, SUB, LANES), 1)
    after = jnp.where(row == SUB - 1, 0.0, pltpu.roll(cells, SUB - 1, 1))
    before = jnp.where(row == 0, 0.0, pltpu.roll(cells, 1, 1))
    return pltpu.roll(jnp.where(lane == 0, after, cells), LANES - 1, 2) + pltpu.roll(
        jnp.where(lane == LANES - 1, before, cells), 1, 2
    )


def split_cells(values):
    high = values.astype(jnp.bfloat16)
    low = (values - high.astype(jnp.float32)).astype(jnp.bfloat16)
    return high, low


def weights(couple_ref):
    high, low = split_cells(couple_ref[...])
    return jnp.concatenate([high, high, low], axis=0)


def advance(src, dst, conduct, code, weight, first, count, low, high):
    rows = high - low
    at = pl.ds(low * SUB, rows * SUB)
    mid = pl.ds(first + 1, count)
    here = src[mid, at, :]
    around = (
        src[pl.ds(first, count), at, :]
        + src[pl.ds(first + 2, count), at, :]
        + src[mid, pl.ds((low - 1) * SUB, rows * SUB), :]
        + src[mid, pl.ds((low + 1) * SUB, rows * SUB), :]
    )
    along = span_sum(here.reshape(count * rows, SUB, LANES)).reshape(here.shape)
    flat = here.reshape(count * rows * SUB, LANES)
    near, rest = split_cells(flat)
    product = jnp.dot(
        jnp.concatenate([near, rest, near], axis=1), weight, preferred_element_type=jnp.float32
    )
    plane = pl.ds(first, count)
    marks = code[plane, at, :]
    penalty = jnp.where(
        marks == 1.0,
        product[:, :LANES].reshape(here.shape),
        jnp.where(marks == 2.0, product[:, LANES:].reshape(here.shape), 0.0),
    )
    dst[mid, at, :] = here + conduct[plane, at, :] * (around + along - 6.0 * here) - penalty


def advance_groups(src, dst, conduct, code, weight, groups, count, stride, low, high):
    for i in range(groups):
        advance(src, dst, conduct, code, weight, i * stride, count, low, high)


def inside(axis):
    place = lax.axis_index(axis)
    return place > 0, place < lax.axis_size(axis) - 1


def kept_if(flag, values):
    return jnp.where(flag, values, 0.0)


def odd_place(axis):
    return lax.axis_index(axis) % 2 == 1


def send(first, second, at, upward, downward, axis="xy"):
    odd = odd_place(axis)
    first[at] = jnp.where(odd, upward, downward)
    second[at] = jnp.where(odd, downward, upward)


def got(first, second, at, from_before, axis="xy"):
    return jnp.where(odd_place(axis) == from_before, second[at], first[at])


def spread(block, dst, offset, at_plane, planes=range(PLANES)):
    for plane in planes:
        for chunk in range(CHUNKS):
            dst[plane + at_plane, pl.ds(offset * SUB + chunk, OWN, stride=SUB), :] = block[
                plane, :, chunk * LANES : (chunk + 1) * LANES
            ]


def widened(codes):
    tile_of = lax.broadcasted_iota(jnp.int32, (LANES, CHUNKS * LANES), 0)
    cell_of = lax.broadcasted_iota(jnp.int32, (LANES, CHUNKS * LANES), 1)
    widen = jnp.where(tile_of == cell_of // TILE, 1.0, 0.0).astype(jnp.bfloat16)
    flat = codes.reshape(-1, LANES).astype(jnp.bfloat16)
    wide = jnp.dot(flat, widen, preferred_element_type=jnp.float32)
    return wide.reshape(codes.shape[0], OWN, CHUNKS * LANES)


def ghosts(src, low, high, from_below=None, from_above=None):
    at = span(low, high)
    if from_below is None:
        src[0, at, :] = src[1, at, :] * 0.6
        src[PLANES + 1, at, :] = src[PLANES, at, :] * 0.6
    else:
        src[0, at, :] = (from_below + 0.75 * src[1, at, :]) * 0.8
        src[PLANES + 1, at, :] = (from_above + 0.75 * src[PLANES, at, :]) * 0.8


def put_traces(src, first, second, level):
    at = span(*reach(level))
    place = trace_place(level)
    to_below = 0.75 * src[2, at, :] - 0.25 * src[1, at, :]
    to_above = 0.75 * src[PLANES - 1, at, :] - 0.25 * src[PLANES, at, :]
    send(first, second, place, to_above, to_below, "zg")


def prepare_kernel(start_field, diffusivity, first, second, own_v, own_d, field, conduct, arrived):
    half = PLANES // 2
    loads = []
    for part in range(2):
        at = pl.ds(part * half, half)
        for source, target in ((start_field, own_v), (diffusivity, own_d)):
            load = pltpu.make_async_copy(source.at[at], target.at[at], arrived.at[len(loads)])
            load.start()
            loads.append(load)
    for part in range(2):
        planes = range(part * half, part * half + half)
        loads[2 * part].wait()
        spread(own_v, field, 0, 0, planes)
        loads[2 * part + 1].wait()
        spread(own_d, conduct, 0, 0, planes)
        for plane in planes:
            at = plane * NEAR
            send(first, second, pl.ds(at, HALF), field[plane, HALF:, :], field[plane, :HALF, :])
            send(
                first, second, pl.ds(at + HALF, REST),
                conduct[plane, OWN_ROWS - REST :, :], conduct[plane, :REST, :],
            )


def code_kernel(tile_block, material, first, second, code, tiles):
    tiles[...] = jnp.zeros(tiles.shape, jnp.int32)
    tiles[:, :, : tile_block.shape[2]] = tile_block[...]
    table = material[...]
    row = lax.broadcasted_iota(jnp.int32, (SUB, LANES), 0)
    bits = jnp.zeros((SUB, LANES), jnp.int32)
    for part in range(table.shape[0] // SUB):
        bits = bits + (table[part * SUB : (part + 1) * SUB] << (row + part * SUB))
    for shift in (4, 2, 1):
        bits = bits + pltpu.roll(bits, shift, 0)
    for plane in range(PLANES):
        block = tiles[plane]
        entry = jnp.maximum(block - 1, 0)
        word = jnp.take_along_axis(bits, entry & (LANES - 1), axis=1)
        kind = (word >> (entry >> 7)) & 1
        code[plane] = jnp.where(block > 0, kind + 1, 0).astype(jnp.float32)
        send(first, second, pl.ds(3 * plane, 3), code[plane, 5:, :], code[plane, :3, :])
    for packet in (first, second):
        packet[3 * PLANES :, :] = jnp.zeros((4, LANES), jnp.float32)


def own_kernel(
    start_field, diffusivity, code, couple,
    field, factor, marks, inner_1, inner_2, inner_3,
    even, odd, wide,
):
    own = pl.ds(OWN_AT, OWN_ROWS)
    spread(start_field, even, HALO, 1)
    spread(diffusivity, factor, HALO, 0)
    wide[...] = widened(code[...])
    spread(wide, marks, HALO, 0)
    field[...] = even[1 : PLANES + 1, own, :]
    weight = weights(couple)
    buffers = (even, odd)
    for level, inner in enumerate((inner_1, inner_2, inner_3)):
        src, dst = buffers[level % 2], buffers[1 - level % 2]
        low, high = HALO + 1 + level, HALO + OWN - 1 - level
        ghosts(src, low, high)
        advance(src, dst, factor, marks, weight, 0, PLANES, low, high)
        inner[...] = dst[1 : PLANES + 1, span(low, high), :]


def keep(src, kept, places, level):
    low, high = reach(level)
    at = span(low - 1, high + 1)
    for plane in range(PLANES):
        if (level, plane) in places:
            kept[places[level, plane], at, :] = src[plane + 1, at, :]


def first_kernel(
    near_first, near_second, code_first, code_second,
    field, conduct, code, inner_1, inner_2, inner_3, couple,
    first, second, trace_first, trace_second, state, kept, factor, marks,
    even, odd, wide, codes,
):
    weight = weights(couple)
    has_left, has_right = inside("xy")
    own = pl.ds(OWN_AT, OWN_ROWS)
    for flag, from_left, offset, near_at, rest_at, place in (
        (has_left, True, 0, 4 * SUB, 5 * SUB, 5),
        (has_right, False, HALO + OWN, 16 * SUB, 16 * SUB, 0),
    ):
        def packet(at, size):
            return kept_if(flag, got(near_first, near_second, pl.ds(at, size), from_left))

        codes[...] = jnp.zeros(codes.shape, jnp.float32)
        for plane in range(PLANES):
            at = plane * NEAR
            even[plane + 1, pl.ds(near_at, HALF), :] = packet(at, HALF)
            factor[plane, pl.ds(rest_at, REST), :] = packet(at + HALF, REST)
            codes[plane, place : place + 3, :] = kept_if(
                flag, got(code_first, code_second, pl.ds(3 * plane, 3), from_left)
            )
        wide[...] = widened(codes[...])
        spread(wide, marks, offset, 0)
    even[1 : PLANES + 1, own, :] = field[...]
    factor[:, own, :] = conduct[:, own, :]
    marks[:, own, :] = code[:, own, :]
    buffers = (even, odd)
    for level in range(SIDE):
        src, dst = buffers[level % 2], buffers[1 - level % 2]
        put_traces(src, trace_first, trace_second, level)
        keep(src, kept, EARLY_KEPT, level)
        low, high = reach(level)
        ghosts(src, low, high)
        for outer in (low, high - SIDE):
            advance_groups(src, dst, factor, marks, weight, 2, 6, 6, outer, outer + SIDE)
        if level < SIDE - 1:
            inner = (inner_1, inner_2, inner_3)[level]
            dst[1 : PLANES + 1, span(low + SIDE, high - SIDE), :] = inner[...]
    state[...] = even[1 : PLANES + 1, OWN_AT : OWN_AT + OWN_ROWS, :]
    for plane in range(PLANES):
        rows = RENEWED[plane] * SUB
        send(
            first, second, pl.ds(RENEWED_AT[plane], rows),
            state[plane, OWN_ROWS - rows :, :], state[plane, :rows, :],
        )


def inner_kernel(state, factor, marks, couple, inner_1, inner_2, inner_3, even, odd):
    weight = weights(couple)
    even[1 : PLANES + 1, pl.ds(OWN_AT, OWN_ROWS), :] = state[...]
    buffers = (even, odd)
    for step, inner in enumerate((inner_1, inner_2, inner_3)):
        src, dst = buffers[step % 2], buffers[1 - step % 2]
        low, high = HALO + 1 + step, HALO + OWN - 1 - step
        ghosts(src, low, high)
        groups, count, stride = ((3, 4, 4), (2, 3, 9), (2, 2, 10))[step]
        advance_groups(src, dst, factor, marks, weight, groups, count, stride, low, high)
        for i in range(groups):
            plane = i * stride
            inner[plane : plane + count] = dst[plane + 1 : plane + 1 + count, span(low, high), :]


def middle_kernel(
    first, second, state, inner_1, inner_2, inner_3, factor, marks, couple,
    trace_first, trace_second, kept,
    even, odd,
):
    weight = weights(couple)
    has_left, has_right = inside("xy")
    for plane in range(PLANES):
        rows = RENEWED[plane] * SUB
        at = pl.ds(RENEWED_AT[plane], rows)
        even[plane + 1, pl.ds(5 * SUB, REST), :] = jnp.zeros((REST, LANES), jnp.float32)
        even[plane + 1, pl.ds(16 * SUB, REST), :] = jnp.zeros((REST, LANES), jnp.float32)
        even[plane + 1, pl.ds(OWN_AT, OWN_ROWS), :] = state[plane]
        even[plane + 1, pl.ds(OWN_AT - rows, rows), :] = kept_if(has_left, got(first, second, at, True))
        even[plane + 1, pl.ds(16 * SUB, rows), :] = kept_if(has_right, got(first, second, at, False))
    buffers = (even, odd)
    for level in range(SIDE, STEPS):
        src, dst = buffers[level % 2], buffers[1 - level % 2]
        put_traces(src, trace_first, trace_second, level)
        keep(src, kept, LATE_KEPT, level)
        if level == STEPS - 1:
            break
        low, high = reach(level)
        ghosts(src, low + 1, high - 1)
        count = STEPS - level
        inner = (inner_1, inner_2, inner_3)[level - SIDE]
        for outer in (low + 1, high - SIDE):
            advance_groups(src, dst, factor, marks, weight, 2, count, PLANES - count, outer, outer + 3)
        parts = [(0, count), (PLANES - count, count)]
        if level == SIDE:
            for outer in (low, high - SIDE):
                advance(src, dst, factor, marks, weight, 5, 2, outer, outer + SIDE)
            parts.append((5, 2))
        for plane, size in parts:
            dst[plane + 1 : plane + 1 + size, span(low + SIDE, high - SIDE), :] = inner[plane : plane + size]


def second_steps(levels, buffers, kept, places, trace_first, trace_second, factor, marks, weight):
    has_below, has_above = inside("zg")
    for level in levels:
        src, dst = buffers[level % 2], buffers[1 - level % 2]
        low, high = reach(level)
        for plane in range(PLANES):
            if (level, plane) in places:
                at = span(low - 1, high + 1)
                src[plane + 1, at, :] = kept[places[level, plane], at, :]
        place = trace_place(level)
        ghosts(
            src, low, high,
            kept_if(has_below, got(trace_first, trace_second, place, True, "zg")),
            kept_if(has_above, got(trace_first, trace_second, place, False, "zg")),
        )
        groups, count, stride = (2, level + 1, 11 - level) if level < 5 else (3, 4, 4)
        advance_groups(src, dst, factor, marks, weight, groups, count, stride, low, high)


def second_kernel(
    trace_first, trace_second, kept, factor, marks, couple,
    first, second, state,
    even, odd,
):
    second_steps(range(SIDE), (even, odd), kept, EARLY_KEPT, trace_first, trace_second, factor, marks, weights(couple))
    for i, plane in enumerate(EDGE_PLANES):
        state[i] = even[plane + 1, pl.ds(OWN_AT, OWN_ROWS), :]
        send(first, second, i, state[i, HALF:, :], state[i, :HALF, :])


def last_kernel(
    trace_first, trace_second, first, second, state, kept, factor, marks, couple,
    result,
    even, odd,
):
    has_left, has_right = inside("xy")
    for i, plane in enumerate(EDGE_PLANES):
        even[plane + 1, pl.ds(OWN_AT, OWN_ROWS), :] = state[i]
        even[plane + 1, pl.ds(OWN_AT - HALF, HALF), :] = kept_if(has_left, got(first, second, i, True))
        even[plane + 1, pl.ds(OWN_AT + OWN_ROWS, HALF), :] = kept_if(has_right, got(first, second, i, False))
    second_steps(
        range(SIDE, STEPS), (even, odd), kept, LATE_KEPT, trace_first, trace_second, factor, marks,
        weights(couple),
    )
    for plane in range(PLANES):
        for chunk in range(CHUNKS):
            result[plane, :, chunk * LANES : (chunk + 1) * LANES] = even[
                plane + 1, pl.ds(OWN_AT + chunk, OWN, stride=SUB), :
            ]


def shape(*dims):
    return jax.ShapeDtypeStruct(dims, jnp.float32)


VMEM = pl.BlockSpec(memory_space=pltpu.VMEM)
HBM = pl.BlockSpec(memory_space=pltpu.HBM)
FIELD = (PLANES, ROWS * SUB, LANES)
PADDED = (PLANES + 2, ROWS * SUB, LANES)
CELLS = (PLANES, OWN_ROWS, LANES)
TRACES = (TRACE_AT[-1], LANES)
WIDE = (PLANES, OWN, CHUNKS * LANES)
PACKET = (PLANES * NEAR, LANES)
CODES = (3 * PLANES + 4, LANES)
SHARE = (RENEWED_AT[-1], LANES)
EDGE_SHARE = (len(EDGE_PLANES), HALF, LANES)


def call(kernel, outs, scratch, *operands, place=VMEM, limit=VMEM_LIMIT):
    return pl.pallas_call(
        kernel,
        out_shape=[shape(*dims) for dims in outs],
        in_specs=[place] * len(operands),
        out_specs=[VMEM] * len(outs),
        scratch_shapes=scratch,
        compiler_params=pltpu.CompilerParams(vmem_limit_bytes=limit),
        name=kernel.__name__,
    )(*operands)


def scratch(*shapes):
    return [pltpu.VMEM(dims, jnp.float32) for dims in shapes]


def swap(first, second, axis):
    levels, lines = lax.axis_size("zg"), lax.axis_size("xy")
    count = lax.axis_size(axis)

    def device(along, other):
        return along * lines + other if axis == "zg" else other * lines + along

    shifted, pairs = [], []
    for other in range(levels * lines // count):
        shifted += [(device(i, other), device(i + 1, other)) for i in range(1, count - 1, 2)]
        pairs += [(device(i, other), device(i + 1, other)) for i in range(0, count, 2)]
        idle = other ^ 1 if axis == "zg" else other ^ 4
        if idle > other:
            shifted += [(device(i, other), device(i, idle)) for i in (0, count - 1)]
    return tuple(
        lax.ppermute(cells, ("zg", "xy"), pairing + [(j, i) for i, j in pairing])
        for cells, pairing in ((first, shifted), (second, pairs))
    )


def on_device(start_field, diffusivity, tile_block, block_material, material_coupling):
    turned = jnp.swapaxes(material_coupling, 1, 2)
    empty = jnp.zeros((TILE, TILE), jnp.float32)
    couple = jnp.concatenate(
        [jnp.block([[turned[kind], empty], [empty, turned[kind]]]) for kind in (0, 1)], axis=1
    )
    material = block_material.reshape(-1, LANES)
    first, second = call(
        prepare_kernel,
        [PACKET, PACKET],
        scratch(start_field.shape, diffusivity.shape, CELLS, CELLS) + [pltpu.SemaphoreType.DMA((4,))],
        start_field, diffusivity,
        place=HBM,
        limit=PREPARE_LIMIT,
    )
    near = swap(first, second, "xy")
    first, second, code = call(
        code_kernel,
        [CODES, CODES, (PLANES, OWN, LANES)],
        [pltpu.VMEM((PLANES, OWN, LANES), jnp.int32)],
        tile_block, material,
    )
    codes = swap(first, second, "xy")
    field, conduct, code, *inner = call(
        own_kernel,
        [CELLS, FIELD, FIELD] + [(PLANES, (OWN - 2 * level) * SUB, LANES) for level in (1, 2, 3)],
        scratch(PADDED, PADDED, WIDE),
        start_field, diffusivity, code, couple,
    )
    first, second, trace_first, trace_second, state, early_kept, factor, marks = call(
        first_kernel,
        [SHARE, SHARE, TRACES, TRACES, CELLS, (len(EARLY_KEPT), ROWS * SUB, LANES), FIELD, FIELD],
        scratch(PADDED, PADDED, WIDE, (PLANES, OWN, LANES)),
        *near, *codes, field, conduct, code, *inner, couple,
    )
    sides = swap(first, second, "xy")
    early = swap(trace_first, trace_second, "zg")
    inner = call(
        inner_kernel,
        [(PLANES, (OWN - 2 * step) * SUB, LANES) for step in (1, 2, 3)],
        scratch(PADDED, PADDED),
        state, factor, marks, couple,
    )
    trace_first, trace_second, late_kept = call(
        middle_kernel,
        [TRACES, TRACES, (len(LATE_KEPT), ROWS * SUB, LANES)],
        scratch(PADDED, PADDED),
        *sides, state, *inner, factor, marks, couple,
    )
    late = swap(trace_first, trace_second, "zg")
    first, second, state = call(
        second_kernel,
        [EDGE_SHARE, EDGE_SHARE, (len(EDGE_PLANES), OWN_ROWS, LANES)],
        scratch(PADDED, PADDED),
        *early, early_kept, factor, marks, couple,
    )
    sides = swap(first, second, "xy")
    (result,) = call(
        last_kernel,
        [start_field.shape],
        scratch(PADDED, PADDED),
        *late, *sides, state, late_kept, factor, marks, couple,
    )
    return result


def solution(mesh):
    return jax.shard_map(
        on_device,
        mesh=mesh,
        in_specs=(P("zg", "xy", None), P("zg", "xy", None), P("zg", "xy", None), P(), P()),
        out_specs=P("zg", "xy", None),
        check_vma=False,
    )
```
